128 devices in a mesh: section: 4 (over x), ctx: 32 (over z, y, core).
Axes of the slice: x: 4, y: 4, z: 4, core: 2. Of those that a mesh axis runs over, the one named last changes fastest.
Arguments:
- queries: bfloat16 [4, 4096, 4096], P('section', 'ctx'), may hold values from -135 to 135
- key_rows: bfloat16 [4, 4096, 512], P('section', 'ctx'), may hold values from -5.1 to 5.1
- value_rows: bfloat16 [4, 4096, 512], P('section', 'ctx'), may hold values from -6 to 6
- out_grad: bfloat16 [4, 4096, 4096], P('section', 'ctx'), may hold values from -6 to 6
- kv_weight: bfloat16 [4, 8192, 1024], P('section', 'ctx'), may hold values from -0.0625 to 0.0625
- doc_lengths: int32 [16], replicated, may hold values from 1 to 1024, 4096 in all
- block_plan: int32 [32], replicated, may hold values from 0 to 31, each once
Outputs:
- query_grad: bfloat16 [4, 4096, 4096], P('section', 'ctx')
- input_grad: bfloat16 [4, 4096, 8192], P('section', 'ctx')
The draws below stay inside these ranges and needn't reach their ends.
Inputs may be any that keep to these rules, and one draw needn't show every extreme that they name: `doc_lengths`: the 16 lengths sum to 4096 and the largest is exactly 1024. `block_plan`: every block number appears exactly once.
All inputs are finite; a program needn't handle non-finite values.
Results may differ from the reference program's by a relative error of at most 0.014.
Values may be sent and summed in bfloat16 or wider, within the bound.
A program may use at most 128 MiB of HBM per device.

```python
import math
import jax
import jax.numpy as jnp
import numpy as np
from jax import lax

D = 8192
HQ = 32
HK = 4
HD = 128
BLOCK = 128
TOK_DEV = 128
TOKENS = 4096
NBLK = 32
MAXDOC = 1024
NDOC = 16
N_SECTION = 4
N_CTX = 32


def shared_keys(key):
    base_keys = jax.random.normal(key, (N_SECTION, TOKENS, HK * HD), jnp.float32)
    return jnp.clip(base_keys, -5.0, 5.0)


def draw_key_rows(key, part):
    base_keys = shared_keys(key)
    return base_keys.astype(jnp.bfloat16)


def draw_queries(key, part):
    key = jax.random.fold_in(key, 5)
    drawn = jnp.clip(jax.random.normal(key, (N_SECTION, TOKENS, HQ * HD), jnp.float32), -6.0, 6.0)
    return drawn.astype(jnp.bfloat16)


def level_of(rng, extent, shards, least, top_value):
    def one(position, parts):
        draws = jax.random.uniform(jax.random.fold_in(jax.random.fold_in(rng, 6), position), (parts,), jnp.float32, least / len(shards), top_value / len(shards))
        return jnp.repeat(jnp.exp(draws), extent[position] // parts).reshape((-1,) + (1,) * (len(extent) - position - 1))

    level = one(*shards[0])
    for cut in shards[1:]:
        level = level * one(*cut)
    return level


def split_up(amount, total, limit, lean):
    loads = [(1 << 20) // math.isqrt(standing ** lean) + 1 for standing in range(2, amount + 1)]
    surplus, given = total - limit - (amount - 1), [1] * (amount - 1)
    while surplus > 0:
        movable = [i for i in range(amount - 1) if given[i] < limit]
        whole, remaining = sum([loads[i] for i in movable]), surplus
        for i in movable:
            more = min(limit - given[i], max(1, remaining * loads[i] // whole), surplus)
            given[i] = given[i] + more
            surplus = surplus - more
    return np.array([limit] + given)


def uneven_parts(stream_key, count, total, bound, slope):
    if count == 2:
        one = jax.random.randint(stream_key, (), max(1, total - bound), min(bound, total - 1) + 1)
        return jnp.stack([one, total - one])
    lengths = jnp.asarray(split_up(count, total, bound, slope), jnp.int32)
    twos = (count - 1) // 2
    source_of, taker = lengths[1:1 + 2 * twos:2], lengths[2:2 + 2 * twos:2]
    margin = jnp.minimum(source_of - 1, bound - taker)
    passed = jax.random.randint(jax.random.fold_in(stream_key, 1), (twos,), 0, 1 << 20) % (margin + 1)
    lengths = lengths.at[1:1 + 2 * twos:2].set(source_of - passed).at[2:2 + 2 * twos:2].set(taker + passed)
    return lengths[jax.random.permutation(jax.random.fold_in(stream_key, 2), count)]


def centred(stream_key, dims, scale, bound, cuts=(), kind=jnp.bfloat16):
    entries = scale * jax.random.normal(stream_key, dims, jnp.float32)
    if cuts:
        entries = entries * level_of(stream_key, dims, cuts, -0.22, 0.18)
    return jnp.clip(entries, -bound, bound).astype(kind)


def setup_inputs(seed: int = 0) -> dict:
    key_of = jax.random.split(jax.random.key(seed), 8)
    queries = draw_queries(jax.random.fold_in(key_of[7], 71), 0)
    key_rows = draw_key_rows(jax.random.fold_in(key_of[7], 71), 0)
    value_rows = centred(key_of[2], (N_SECTION, TOKENS, HK * HD), 1.0, 6.0, ((0, 4), (1, 32)))
    out_grad = centred(key_of[3], (N_SECTION, TOKENS, HQ * HD), 1.0, 6.0, ((0, 4), (1, 32)))
    kv_weight = centred(key_of[4], (N_SECTION, D, 2 * HK * HD), D ** -0.5, 0.0625, ((0, 4), (1, 32)))
    doc_lengths = uneven_parts(key_of[5], NDOC, TOKENS, MAXDOC, 2).astype(jnp.int32)
    block_plan = jax.random.permutation(key_of[6], NBLK).astype(jnp.int32)
    return {"queries": queries, "key_rows": key_rows, "value_rows": value_rows, "out_grad": out_grad, "kv_weight": kv_weight, "doc_lengths": doc_lengths, "block_plan": block_plan}


MASKED_SCORE = -1e+30

def token_layout(block_plan, doc_lengths):
    within = jnp.arange(BLOCK, dtype=jnp.int32)
    token_ids = (block_plan[:, None] * BLOCK + within[None, :]).reshape(-1).astype(jnp.int32)
    doc_ends = jnp.cumsum(doc_lengths).astype(jnp.int32)
    doc_ids = lax.optimization_barrier(jnp.sum((token_ids[:, None] >= doc_ends[None, :]).astype(jnp.int32), axis=1))
    return (token_ids, doc_ids)

def section_grads(queries, key_rows, value_rows, out_grad, kv_weight, token_ids, doc_ids):
    total_rows = key_rows.shape[0]
    group_size = HQ // HK
    score_scale = 1.0 / math.sqrt(HD)
    highest = lax.Precision.HIGHEST
    keys_all = key_rows.astype(jnp.float32).reshape(total_rows, HK, HD)
    values_all = value_rows.astype(jnp.float32).reshape(total_rows, HK, HD)
    query_all = queries.astype(jnp.float32).reshape(N_CTX, TOK_DEV, HK, group_size, HD)
    grad_all = out_grad.astype(jnp.float32).reshape(N_CTX, TOK_DEV, HK, group_size, HD)
    tokens_blocked = token_ids.reshape(N_CTX, TOK_DEV)
    docs_blocked = doc_ids.reshape(N_CTX, TOK_DEV)

    def per_group(summed, inputs):
        query_heads, grad_heads, row_tokens, row_docs = inputs
        visible_mask = jnp.logical_and(row_docs[:, None] == doc_ids[None, :], token_ids[None, :] <= row_tokens[:, None])
        scores = jnp.einsum('qkgd,skd->kgqs', query_heads, keys_all, precision=highest) * score_scale
        masked = jnp.where(visible_mask, scores, MASKED_SCORE)
        row_peak = lax.optimization_barrier(jnp.max(masked, axis=-1))
        weight_sum = lax.optimization_barrier(jnp.sum(jnp.where(visible_mask, jnp.exp(masked - row_peak[..., None]), 0.0), axis=-1))
        log_total = row_peak + jnp.log(weight_sum)
        prob = jnp.where(visible_mask, jnp.exp(masked - log_total[..., None]), 0.0)
        grad_prob = jnp.einsum('qkgd,skd->kgqs', grad_heads, values_all, precision=highest)
        delta = lax.optimization_barrier(jnp.sum(prob * grad_prob, axis=-1))
        grad_score = prob * (grad_prob - delta[..., None])
        prob_low = lax.optimization_barrier(prob.astype(jnp.bfloat16)).astype(jnp.float32)
        score_low = lax.optimization_barrier(grad_score.astype(jnp.bfloat16)).astype(jnp.float32)
        value_grad = jnp.einsum('kgqs,qkgd->skd', prob_low, grad_heads, precision=highest)
        key_grad = jnp.einsum('kgqs,qkgd->skd', score_low, query_heads, precision=highest) * score_scale
        query_grad = jnp.einsum('kgqs,skd->qkgd', score_low, keys_all, precision=highest) * score_scale
        partial_term = jnp.concatenate([key_grad.reshape(total_rows, HK * HD), value_grad.reshape(total_rows, HK * HD)], axis=1)
        rounded = lax.optimization_barrier(partial_term.astype(jnp.bfloat16)).astype(jnp.float32)
        return (summed + rounded, query_grad.reshape(TOK_DEV, HQ * HD).astype(jnp.bfloat16))
    start_sum = jnp.zeros((total_rows, 2 * HK * HD), jnp.float32)
    kv_sum, query_blocks = lax.scan(per_group, start_sum, (query_all, grad_all, tokens_blocked, docs_blocked))
    kv_grad = kv_sum.astype(jnp.bfloat16)
    local_input = jnp.dot(kv_grad, kv_weight.T, preferred_element_type=jnp.float32).astype(jnp.bfloat16)
    return (query_blocks.reshape(total_rows, HQ * HD), local_input)

def reference(queries, key_rows, value_rows, out_grad, kv_weight, doc_lengths, block_plan):
    token_ids, doc_ids = token_layout(block_plan, doc_lengths)
    query_list = []
    input_list = []
    for section_index in range(N_SECTION):
        query_grad, local_input = section_grads(queries[section_index], key_rows[section_index], value_rows[section_index], out_grad[section_index], kv_weight[section_index], token_ids, doc_ids)
        query_list.append(query_grad)
        input_list.append(local_input)
    return (jnp.stack(query_list), jnp.roll(jnp.stack(input_list), -1, axis=0))
```

```python
import functools
import math

import jax
import jax.numpy as jnp
from jax import lax
from jax.experimental import pallas as pl
from jax.experimental.pallas import tpu as pltpu
from jax.sharding import PartitionSpec as P

HQ = 32
HK = 4
HD = 128
BLOCK = 128
GROUP = HQ // HK
BACK = 8
SLOTS = BACK + 1
CH = 2 * HK
SUB = 32
RG = BLOCK // SUB
MASKED = -1e30
MESH = pl.DeviceIdType.MESH


def rem(a, b):
    return lax.rem(a, b)


def div(a, b):
    return lax.div(a, b)


def kernel(
    n, sections, lens, plan, inv, q_hbm, k_ref, v_ref, o_hbm, w_hbm, dq_hbm, out_hbm,
    q_s, o_s, dq_s, kvw, recv1, send2, bias, dk_acc, dv_acc, part, recv3, kvo, kvg, wsh, wfull, outs,
    in_sem, dq_sem, s1s, s1r, s2s, s2r, s3s, s3r, xs, xr, gs, gr, os_, or_, loc_sem, wxs, wxr, wgs, wgr,
):
    me = lax.axis_index("ctx")
    sec = lax.axis_index("section")
    rg = div(me, CH)
    ch = rem(me, CH)
    before = rem(sec + sections - 1, sections)

    def remote(src, dst, send, recv, **where):
        return pltpu.make_async_remote_copy(
            src_ref=src, dst_ref=dst, send_sem=send, recv_sem=recv,
            device_id=where, device_id_type=MESH,
        )

    def rows(group):
        return pl.ds(pl.multiple_of(group * SUB, SUB), SUB)

    def others(body):
        def step(k, carry):
            body(rem(me + k, n))
            return carry
        lax.fori_loop(1, n, step, 0)

    load_q = pltpu.make_async_copy(q_hbm, q_s, in_sem.at[0])
    load_o = pltpu.make_async_copy(o_hbm, o_s, in_sem.at[1])
    load_q.start()
    load_o.start()

    barrier = pltpu.get_barrier_semaphore()
    others(lambda j: pl.semaphore_signal(barrier, inc=1, device_id={"ctx": j}, device_id_type=MESH))
    pl.semaphore_signal(barrier, inc=1, device_id={"section": rem(sec + 1, sections)}, device_id_type=MESH)
    for head in range(HK):
        kvw[head, BACK] = k_ref[:, head * HD:(head + 1) * HD]
        kvw[HK + head, BACK] = v_ref[:, head * HD:(head + 1) * HD]
    pl.semaphore_wait(barrier, n)

    def piece_out(j):
        return remote(kvw.at[rem(j, CH), BACK, rows(div(j, CH))], recv1.at[me], s1s.at[j], s1r.at[me], ctx=j)

    others(lambda j: piece_out(j).start())
    w_shift = remote(w_hbm, wsh, wxs, wxr, section=before)
    w_shift.start()
    recv1[me] = kvw[ch, BACK, rows(rg)]

    token_block = plan[me]
    row_token = token_block * BLOCK + lax.broadcasted_iota(jnp.int32, (1, BLOCK), 1)
    start = jnp.zeros((1, BLOCK), jnp.int32)
    end = jnp.int32(0)
    for j in range(lens.shape[0]):
        end = end + lens[j]
        start = jnp.where(row_token >= end, end, start)
    key_token = (token_block - BACK) * BLOCK + lax.broadcasted_iota(jnp.int32, (SLOTS * BLOCK, BLOCK), 0)
    seen = jnp.logical_and(key_token >= start, key_token <= row_token)
    bias[...] = jnp.where(seen, 0.0, MASKED)

    def piece_in(j):
        return remote(kvw.at[0, BACK, rows(0)], recv1.at[j], s1s.at[j], s1r.at[j], ctx=j)

    others(lambda j: piece_in(j).wait_recv())

    def window_out(d):
        return remote(send2.at[d], kvw.at[ch, pl.ds(0, BACK), rows(rg)], s2s.at[d], s2r.at[me], ctx=d)

    def window_send(d):
        first = plan[d] - BACK
        for w in range(BACK):
            send2[d, w] = recv1[inv[jnp.maximum(first + w, 0)]]
        window_out(d).start()

    others(window_send)
    for w in range(BACK):
        kvw[ch, w, rows(rg)] = recv1[inv[jnp.maximum(token_block - BACK + w, 0)]]

    def window_in(j):
        return remote(send2.at[j], kvw.at[rem(j, CH), pl.ds(0, BACK), rows(div(j, CH))], s2s.at[j], s2r.at[j], ctx=j)

    others(lambda j: window_in(j).wait_recv())

    w_shift.wait_recv()
    w_slot = rem(me, RG)

    def w_rows(slot):
        return wfull.at[pl.ds(pl.multiple_of(slot * w_hbm.shape[0], 256), w_hbm.shape[0])]

    def w_target(z):
        return z * CH + div(me, RG)

    for z in range(RG):
        @pl.when(w_target(z) != me)
        def _():
            remote(wsh, w_rows(w_slot), wgs.at[z], wgr.at[w_slot], ctx=w_target(z)).start()

        @pl.when(w_target(z) == me)
        def _():
            pltpu.make_async_copy(wsh, w_rows(w_slot), loc_sem.at[1]).start()

    load_q.wait()
    load_o.wait()

    scale = 1.0 / math.sqrt(HD)
    power = scale * math.log2(math.e)
    nt = (((1,), (1,)), ((), ()))

    def part_out(j):
        return remote(part.at[rem(j, CH), :, rows(div(j, CH))], recv3.at[me], s3s.at[j], s3r.at[me], ctx=j)

    def part_own():
        return pltpu.make_async_copy(part.at[ch, :, rows(rg)], recv3.at[me], loc_sem.at[0])

    def one_head(step, carry):
        head = rem(step + me, HK)
        keys = kvw[head].reshape(SLOTS * BLOCK, HD)
        values = kvw[HK + head].reshape(SLOTS * BLOCK, HD)
        keys_t = keys.T

        def one_pair(pair, carry):
            def columns(i):
                return pl.ds(pl.multiple_of((head * GROUP + pair * 2 + i) * HD, HD), HD)

            q2 = jnp.concatenate([q_s[:, columns(0)], q_s[:, columns(1)]], axis=0)
            o2 = jnp.concatenate([o_s[:, columns(0)], o_s[:, columns(1)]], axis=0)
            b = bias[...]
            scores = lax.dot_general(keys, q2, nt, preferred_element_type=jnp.float32)
            scores = scores + jnp.concatenate([b, b], axis=1)
            grads = lax.dot_general(values, o2, nt, preferred_element_type=jnp.float32)
            peak = jnp.max(scores, axis=0, keepdims=True)
            terms = jnp.exp2((scores - peak) * power)
            inverse = 1.0 / jnp.sum(terms, axis=0, keepdims=True)
            delta = jnp.sum(terms * grads, axis=0, keepdims=True) * inverse
            prob = terms * inverse
            prob_low = prob.astype(jnp.bfloat16)
            score_low = (prob * (grads - delta)).astype(jnp.bfloat16)
            dv = jnp.dot(prob_low, o2, preferred_element_type=jnp.float32)
            dk = jnp.dot(score_low, q2, preferred_element_type=jnp.float32)
            dq_t = jnp.dot(keys_t, score_low, preferred_element_type=jnp.float32) * scale
            dq_s[:, columns(0)] = dq_t[:, :BLOCK].T.astype(jnp.bfloat16)
            dq_s[:, columns(1)] = dq_t[:, BLOCK:].T.astype(jnp.bfloat16)
            keep = jnp.where(pair == 0, 0.0, 1.0)
            dv_acc[...] = dv_acc[...] * keep + dv
            dk_acc[...] = dk_acc[...] * keep + dk
            return carry

        dv_acc[...] = jnp.zeros_like(dv_acc)
        dk_acc[...] = jnp.zeros_like(dk_acc)
        lax.fori_loop(0, GROUP // 2, one_pair, 0)
        part[head] = (dk_acc[...] * scale).astype(jnp.bfloat16).reshape(SLOTS, BLOCK, HD)
        part[HK + head] = dv_acc[...].astype(jnp.bfloat16).reshape(SLOTS, BLOCK, HD)

        def send(i, carry):
            j = div(i, 2) * CH + rem(i, 2) * HK + head

            @pl.when(j != me)
            def _():
                part_out(j).start()

            @pl.when(j == me)
            def _():
                part_own().start()
            return carry

        lax.fori_loop(0, 2 * RG, send, 0)
        wide = pl.ds(pl.multiple_of(head * GROUP * HD, GROUP * HD), GROUP * HD)
        pltpu.make_async_copy(dq_s.at[:, wide], dq_hbm.at[:, wide], dq_sem.at[head]).start()
        return carry

    lax.fori_loop(0, HK, one_head, 0)

    def part_in(j):
        return remote(part.at[0, :, rows(0)], recv3.at[j], s3s.at[j], s3r.at[j], ctx=j)

    others(lambda j: part_in(j).wait_recv())
    part_own().wait()

    per = n // RG

    def blocks(chunk):
        return pl.ds(pl.multiple_of(chunk * per, per), per)

    def x_copy(chunk):
        return remote(kvo.at[blocks(chunk)], kvg.at[ch, blocks(chunk)], xs.at[chunk], xr.at[chunk], section=before)

    def reduce_chunk(step, carry):
        chunk = rem(step + rg, RG)

        def one_block(i, carry):
            p = chunk * per + i
            total = jnp.zeros((SUB, HD), jnp.float32)
            for w in range(SLOTS):
                later = plan[p] + BACK - w
                term = recv3[inv[jnp.minimum(later, n - 1)], w].astype(jnp.float32)
                total = total + jnp.where(later < n, term, 0.0)
            kvo[p] = total.astype(jnp.bfloat16)
            return carry

        lax.fori_loop(0, per, one_block, 0)
        x_copy(chunk).start()
        return carry

    lax.fori_loop(0, RG, reduce_chunk, 0)

    def gather(chunk, source, target):
        return remote(
            kvg.at[source, blocks(chunk)], kvg.at[source, blocks(chunk)],
            gs.at[chunk, target], gr.at[chunk, source], ctx=rg * CH + target,
        )

    def gather_chunk(step, carry):
        chunk = rem(step + rg, RG)
        x_copy(chunk).wait_recv()
        for i in range(1, CH):
            gather(chunk, ch, rem(ch + i, CH)).start()
        return carry

    lax.fori_loop(0, RG, gather_chunk, 0)

    for u in range(RG):
        @pl.when(RG * ch + u != me)
        def _():
            remote(wsh, w_rows(u), wgs.at[u], wgr.at[u], ctx=RG * ch + u).wait_recv()

        @pl.when(RG * ch + u == me)
        def _():
            pltpu.make_async_copy(wsh, w_rows(u), loc_sem.at[1]).wait()

    wide = wfull.shape[0]

    def out_part(group, chunk):
        return out_hbm.at[rows(group), pl.ds(pl.multiple_of(chunk * wide, wide), wide)]

    def out_copy(p):
        return remote(outs.at[p], out_part(rg, ch), os_.at[p], or_.at[me], ctx=p)

    def out_own():
        return pltpu.make_async_copy(outs.at[me], out_part(rg, ch), loc_sem.at[2])

    def multiply_chunk(step, carry):
        chunk = rem(step + rg, RG)
        for i in range(1, CH):
            gather(chunk, rem(ch + i, CH), ch).wait_recv()
        left = jnp.concatenate([kvg[i, blocks(chunk)].reshape(per * SUB, HD) for i in range(CH)], axis=1)
        product = lax.dot_general(left, wfull[...], nt, preferred_element_type=jnp.float32)
        outs[blocks(chunk)] = product.astype(jnp.bfloat16).reshape(per, SUB, wide)

        def send(i, carry):
            p = chunk * per + rem(i + ch, per)

            @pl.when(p != me)
            def _():
                out_copy(p).start()

            @pl.when(p == me)
            def _():
                out_own().start()
            return carry

        lax.fori_loop(0, per, send, 0)
        return carry

    lax.fori_loop(0, RG, multiply_chunk, 0)

    others(lambda j: piece_out(j).wait_send())
    others(lambda j: window_out(j).wait_send())
    others(lambda j: part_out(j).wait_send())
    w_shift.wait_send()
    for z in range(RG):
        @pl.when(w_target(z) != me)
        def _():
            remote(wsh, w_rows(w_slot), wgs.at[z], wgr.at[w_slot], ctx=w_target(z)).wait_send()

    def sent(chunk, carry):
        x_copy(chunk).wait_send()
        for i in range(1, CH):
            gather(chunk, ch, rem(ch + i, CH)).wait_send()
        return carry

    lax.fori_loop(0, RG, sent, 0)
    for head in range(HK):
        wide_q = pl.ds(head * GROUP * HD, GROUP * HD)
        pltpu.make_async_copy(dq_s.at[:, wide_q], dq_hbm.at[:, wide_q], dq_sem.at[head]).wait()
    others(lambda j: out_copy(j).wait_send())
    out_own().wait()
    others(lambda j: remote(outs.at[j], out_part(div(j, CH), rem(j, CH)), os_.at[j], or_.at[j], ctx=j).wait_recv())


def shards(queries, key_rows, value_rows, out_grad, kv_weight, doc_lengths, block_plan):
    n = lax.axis_size("ctx")
    sections = lax.axis_size("section")
    number = jnp.arange(n, dtype=jnp.int32)
    inverse_plan = jnp.sum(jnp.where(block_plan[None, :] == number[:, None], number[None, :], 0), axis=1, dtype=jnp.int32)
    tokens, width = queries.shape[1:]
    features = kv_weight.shape[1]
    model = features * n
    share = model // CH
    per = n // RG
    smem = pl.BlockSpec(memory_space=pltpu.SMEM)
    vmem = pl.BlockSpec(memory_space=pltpu.VMEM)
    hbm = pl.BlockSpec(memory_space=pl.ANY)
    low = jnp.bfloat16
    dma = pltpu.SemaphoreType.DMA
    query_grad, input_grad = pl.pallas_call(
        functools.partial(kernel, n, sections),
        out_shape=(
            jax.ShapeDtypeStruct((tokens, width), low),
            jax.ShapeDtypeStruct((tokens, model), low),
        ),
        in_specs=[smem, smem, smem, hbm, vmem, vmem, hbm, hbm],
        out_specs=(hbm, hbm),
        scratch_shapes=[
            pltpu.VMEM((tokens, width), low),
            pltpu.VMEM((tokens, width), low),
            pltpu.VMEM((tokens, width), low),
            pltpu.VMEM((CH, SLOTS, BLOCK, HD), low),
            pltpu.VMEM((n, SUB, HD), low),
            pltpu.VMEM((n, BACK, SUB, HD), low),
            pltpu.VMEM((SLOTS * BLOCK, BLOCK), jnp.float32),
            pltpu.VMEM((SLOTS * BLOCK, HD), jnp.float32),
            pltpu.VMEM((SLOTS * BLOCK, HD), jnp.float32),
            pltpu.VMEM((CH, SLOTS, BLOCK, HD), low),
            pltpu.VMEM((n, SLOTS, SUB, HD), low),
            pltpu.VMEM((n, SUB, HD), low),
            pltpu.VMEM((CH, n, SUB, HD), low),
            pltpu.VMEM((features, CH * HD), low),
            pltpu.VMEM((share, CH * HD), low),
            pltpu.VMEM((n, SUB, share), low),
            dma((2,)), dma((HK,)),
            dma((n,)), dma((n,)), dma((n,)), dma((n,)), dma((n,)), dma((n,)),
            dma((RG,)), dma((RG,)), dma((RG, CH)), dma((RG, CH)), dma((n,)), dma((n,)),
            dma((3,)), dma, dma, dma((RG,)), dma((RG,)),
        ],
        compiler_params=pltpu.CompilerParams(
            collective_id=0, has_side_effects=True, vmem_limit_bytes=56 * 1024 * 1024
        ),
    )(doc_lengths, block_plan, inverse_plan, queries[0], key_rows[0], value_rows[0], out_grad[0], kv_weight[0])
    return (query_grad[None], input_grad[None])


def solution(mesh):
    spec = P("section", "ctx", None)
    return jax.shard_map(
        shards, mesh=mesh, in_specs=(spec,) * 5 + (P(), P()), out_specs=(spec, spec), check_vma=False
    )
```

```python
import functools
import math

import jax
import jax.numpy as jnp
from jax import lax
from jax.experimental import pallas as pl
from jax.experimental.pallas import tpu as pltpu
from jax.sharding import PartitionSpec as P

HQ = 32
HK = 4
HD = 128
BLOCK = 128
GROUP = HQ // HK
BACK = 8
SLOTS = BACK + 1
CH = 2 * HK
SUB = 32
RG = BLOCK // SUB
MASKED = -1e30
MIX = 13
KEYS = 384
MESH = pl.DeviceIdType.MESH


def rem(a, b):
    return lax.rem(a, b)


def div(a, b):
    return lax.div(a, b)


def kernel(
    n, sections, lens, plan, inv, q_hbm, k_ref, v_ref, o_hbm, w_hbm, dq_hbm, out_hbm,
    q_s, o_s, dq_s, kvw, recv1, send2, bias, s_s, g_s, part, recv3, kvo, kvg, wsh, wfull, outs,
    in_sem, dq_sem, s1s, s1r, s2s, s2r, s3s, s3r, xs, xr, gs, gr, os_, or_, loc_sem, wxs, wxr, wgs, wgr,
):
    me = lax.axis_index("ctx")
    sec = lax.axis_index("section")
    rg = div(me, CH)
    ch = rem(me, CH)
    core = rem(ch, 2)
    column = div(ch, 2)
    before = rem(sec + sections - 1, sections)

    def remote(src, dst, send, recv, **where):
        return pltpu.make_async_remote_copy(
            src_ref=src, dst_ref=dst, send_sem=send, recv_sem=recv,
            device_id=where, device_id_type=MESH,
        )

    def rows(group):
        return pl.ds(pl.multiple_of(group * SUB, SUB), SUB)

    def others(body):
        def step(k, carry):
            body(rem(me + MIX * k, n))
            return carry
        lax.fori_loop(1, n, step, 0)

    load_q = pltpu.make_async_copy(q_hbm, q_s, in_sem.at[0])
    load_o = pltpu.make_async_copy(o_hbm, o_s, in_sem.at[1])
    load_q.start()
    load_o.start()

    barrier = pltpu.get_barrier_semaphore()
    others(lambda j: pl.semaphore_signal(barrier, inc=1, device_id={"ctx": j}, device_id_type=MESH))
    pl.semaphore_signal(barrier, inc=1, device_id={"section": rem(sec + 1, sections)}, device_id_type=MESH)
    for head in range(HK):
        kvw[head, BACK] = k_ref[:, head * HD:(head + 1) * HD]
        kvw[HK + head, BACK] = v_ref[:, head * HD:(head + 1) * HD]
    pl.semaphore_wait(barrier, n)

    def piece_out(j):
        return remote(kvw.at[rem(j, CH), BACK, rows(div(j, CH))], recv1.at[me], s1s.at[j], s1r.at[me], ctx=j)

    others(lambda j: piece_out(j).start())
    w_shift = remote(w_hbm, wsh, wxs, wxr, section=before)
    w_shift.start()
    recv1[me] = kvw[ch, BACK, rows(rg)]

    token_block = plan[me]
    row_token = token_block * BLOCK + lax.broadcasted_iota(jnp.int32, (1, BLOCK), 1)
    start = jnp.zeros((1, BLOCK), jnp.int32)
    end = jnp.int32(0)
    for j in range(lens.shape[0]):
        end = end + lens[j]
        start = jnp.where(row_token >= end, end, start)
    key_token = (token_block - BACK) * BLOCK + lax.broadcasted_iota(jnp.int32, (SLOTS * BLOCK, BLOCK), 0)
    seen = jnp.logical_and(key_token >= start, key_token <= row_token)
    bias[...] = jnp.where(seen, 0.0, MASKED)

    def piece_in(j):
        return remote(kvw.at[0, BACK, rows(0)], recv1.at[j], s1s.at[j], s1r.at[j], ctx=j)

    others(lambda j: piece_in(j).wait_recv())

    def window_out(d):
        return remote(send2.at[d], kvw.at[ch, pl.ds(0, BACK), rows(rg)], s2s.at[d], s2r.at[me], ctx=d)

    head_of = rem(ch, HK)

    def window_own():
        return pltpu.make_async_copy(send2.at[me], kvw.at[ch, pl.ds(0, BACK), rows(rg)], loc_sem.at[0])

    def window_step(i, carry):
        d = HK * rem(div(me, HK) + 3 * i, n // HK) + rem(head_of - div(i, n // HK) + HK, HK)
        first = plan[d] - BACK
        for w in range(BACK):
            send2[d, w] = recv1[inv[jnp.maximum(first + w, 0)]]

        @pl.when(d != me)
        def _():
            window_out(d).start()

        @pl.when(d == me)
        def _():
            window_own().start()
        return carry

    lax.fori_loop(0, n, window_step, 0)

    def window_in(j):
        return remote(send2.at[j], kvw.at[rem(j, CH), pl.ds(0, BACK), rows(div(j, CH))], s2s.at[j], s2r.at[j], ctx=j)

    w_slot = rem(rg, 2) * 2 + core

    def w_rows(slot):
        return wfull.at[pl.ds(pl.multiple_of(slot * w_hbm.shape[0], 256), w_hbm.shape[0])]

    def w_target(z):
        return z * CH + 2 * column + div(rg, 2)

    def w_source(u):
        return (2 * core + u // 2) * CH + 2 * column + u % 2

    def w_out(z):
        return remote(wsh, w_rows(w_slot), wgs.at[z], wgr.at[w_slot], ctx=w_target(z))

    def w_own():
        return pltpu.make_async_copy(wsh, w_rows(w_slot), loc_sem.at[1])

    def spread_weights():
        w_shift.wait_recv()
        for z in range(RG):
            @pl.when(w_target(z) != me)
            def _():
                w_out(z).start()

            @pl.when(w_target(z) == me)
            def _():
                w_own().start()

    load_q.wait()
    load_o.wait()

    scale = 1.0 / math.sqrt(HD)
    power = scale * math.log2(math.e)
    nt = (((1,), (1,)), ((), ()))
    tn = (((0,), (0,)), ((), ()))

    def part_out(j):
        return remote(part.at[rem(j, CH), :, rows(div(j, CH))], recv3.at[me], s3s.at[j], s3r.at[me], ctx=j)

    def part_own():
        return pltpu.make_async_copy(part.at[ch, :, rows(rg)], recv3.at[me], loc_sem.at[2])

    def one_head(step, carry):
        head = rem(step + me, HK)

        def arrived(i, carry):
            j = HK * i + head

            @pl.when(j != me)
            def _():
                window_in(j).wait_recv()

            @pl.when(j == me)
            def _():
                window_own().wait()
            return carry

        lax.fori_loop(0, n // HK, arrived, 0)

        @pl.when(step == 1)
        def _():
            spread_weights()

        def columns(i):
            return pl.ds(pl.multiple_of((head * GROUP + i) * HD, HD), HD)

        q2 = jnp.concatenate([q_s[:, columns(i)] for i in range(GROUP)], axis=0)
        o2 = jnp.concatenate([o_s[:, columns(i)] for i in range(GROUP)], axis=0)
        wide = GROUP * BLOCK
        spans = [(slice(i, i + KEYS), slice(i // BLOCK, (i + KEYS) // BLOCK)) for i in range(0, SLOTS * BLOCK, KEYS)]

        def folded(x, over):
            return over(x.reshape(KEYS // 8, 8, wide), axis=0)

        peak = None
        for span, slots in spans:
            b = bias[span]
            keys = kvw[head, slots].reshape(KEYS, HD)
            scores = lax.dot_general(keys, q2, nt, preferred_element_type=jnp.float32)
            scores = scores + jnp.concatenate([b] * GROUP, axis=1)
            s_s[span] = scores
            top = folded(scores, jnp.max)
            peak = top if peak is None else jnp.maximum(peak, top)
            values = kvw[HK + head, slots].reshape(KEYS, HD)
            g_s[span] = lax.dot_general(values, o2, nt, preferred_element_type=jnp.float32)
        peak = jnp.max(peak, axis=0, keepdims=True)
        total = jnp.zeros((8, wide), jnp.float32)
        weighted = jnp.zeros((8, wide), jnp.float32)
        for span, slots in spans:
            terms = jnp.exp2((s_s[span] - peak) * power)
            s_s[span] = terms
            total = total + folded(terms, jnp.sum)
            weighted = weighted + folded(terms * g_s[span], jnp.sum)
        inverse = 1.0 / jnp.sum(total, axis=0, keepdims=True)
        delta = jnp.sum(weighted, axis=0, keepdims=True) * inverse
        dq = jnp.zeros((wide, HD), jnp.float32)
        for span, slots in spans:
            prob = s_s[span] * inverse
            prob_low = prob.astype(jnp.bfloat16)
            score_low = (prob * (g_s[span] - delta)).astype(jnp.bfloat16)
            dv = jnp.dot(prob_low, o2, preferred_element_type=jnp.float32)
            dk = jnp.dot(score_low, q2, preferred_element_type=jnp.float32) * scale
            part[HK + head, slots] = dv.astype(jnp.bfloat16).reshape(KEYS // BLOCK, BLOCK, HD)
            part[head, slots] = dk.astype(jnp.bfloat16).reshape(KEYS // BLOCK, BLOCK, HD)
            keys = kvw[head, slots].reshape(KEYS, HD)
            dq = dq + lax.dot_general(score_low, keys, tn, preferred_element_type=jnp.float32)
        for i in range(GROUP):
            dq_s[:, columns(i)] = (dq[i * BLOCK:(i + 1) * BLOCK] * scale).astype(jnp.bfloat16)

        def send(i, carry):
            turn = rem(3 * i + div(me, HK), n // HK)
            j = turn * HK + head

            @pl.when(j != me)
            def _():
                part_out(j).start()

            @pl.when(j == me)
            def _():
                part_own().start()
            return carry

        lax.fori_loop(0, 2 * RG, send, 0)
        wide = pl.ds(pl.multiple_of(head * GROUP * HD, GROUP * HD), GROUP * HD)
        pltpu.make_async_copy(dq_s.at[:, wide], dq_hbm.at[:, wide], dq_sem.at[head]).start()
        return carry

    lax.fori_loop(0, HK, one_head, 0)

    def part_in(j):
        return remote(part.at[0, :, rows(0)], recv3.at[j], s3s.at[j], s3r.at[j], ctx=j)

    others(lambda j: part_in(j).wait_recv())
    part_own().wait()

    per = n // RG

    def owner(chunk, i):
        z = div(i, 2)
        return z * CH + 2 * rem(chunk - z + RG, RG) + rem(i, 2)

    def blocks(chunk):
        return pl.ds(pl.multiple_of(chunk * per, per), per)

    def x_copy(chunk):
        return remote(kvo.at[blocks(chunk)], kvg.at[ch, blocks(chunk)], xs.at[chunk], xr.at[chunk], section=before)

    def reduce_chunk(step, carry):
        chunk = rem(step + rg, RG)

        def one_block(i, carry):
            p = owner(chunk, i)
            total = jnp.zeros((SUB, HD), jnp.float32)
            for w in range(SLOTS):
                later = plan[p] + BACK - w
                term = recv3[inv[jnp.minimum(later, n - 1)], w].astype(jnp.float32)
                total = total + jnp.where(later < n, term, 0.0)
            kvo[chunk * per + i] = total.astype(jnp.bfloat16)
            return carry

        lax.fori_loop(0, per, one_block, 0)
        x_copy(chunk).start()
        return carry

    lax.fori_loop(0, RG, reduce_chunk, 0)

    sibling = rg * CH + 2 * column + 1 - core

    def gather(chunk, source, target, slot):
        return remote(
            kvg.at[source, blocks(chunk)], kvg.at[source, blocks(chunk)],
            gs.at[chunk, slot], gr.at[chunk, source], ctx=target,
        )

    def along(i):
        return 2 * rem(column + i, RG)

    def gather_chunk(step, carry):
        chunk = rem(step + rg, RG)
        x_copy(chunk).wait_recv()
        for i in range(1, RG):
            gather(chunk, ch, rg * CH + along(i) + core, i).start()
        gather(chunk, ch, sibling, 0).start()
        return carry

    lax.fori_loop(0, RG, gather_chunk, 0)

    def share_chunk(step, carry):
        chunk = rem(step + rg, RG)
        for i in range(1, RG):
            source = along(i) + core
            gather(chunk, source, sibling, RG + i).wait_recv()
            gather(chunk, source, sibling, RG + i).start()
        return carry

    lax.fori_loop(0, RG, share_chunk, 0)

    for u in range(RG):
        @pl.when(w_source(u) != me)
        def _():
            remote(wsh, w_rows(u), wgs.at[u], wgr.at[u], ctx=w_source(u)).wait_recv()

        @pl.when(w_source(u) == me)
        def _():
            w_own().wait()

    wide = wfull.shape[0] // 2

    def out_part(j, v):
        first = (2 * rem(j, 2) + v) * CH * wide // 2 + rem(div(j, 2), RG) * wide
        return out_hbm.at[rows(div(j, CH)), pl.ds(pl.multiple_of(first, wide), wide)]

    def out_copy(index, p, v):
        return remote(outs.at[v, index], out_part(me, v), os_.at[v, p], or_.at[v, me], ctx=p)

    def out_own(index, v):
        return pltpu.make_async_copy(outs.at[v, index], out_part(me, v), loc_sem.at[3 + v])

    def multiply_chunk(step, carry):
        chunk = rem(step + rg, RG)
        for i in range(RG):
            source = along(i) + 1 - core
            gather(chunk, source, sibling, 0).wait_recv()
        left = jnp.concatenate([kvg[i, blocks(chunk)].reshape(per * SUB, HD) for i in range(CH)], axis=1)
        for v in range(2):
            product = lax.dot_general(left, wfull[v * wide:(v + 1) * wide], nt, preferred_element_type=jnp.float32)
            outs[v, blocks(chunk)] = product.astype(jnp.bfloat16).reshape(per, SUB, wide)

            def send(i, carry):
                turn = rem(3 * i + ch, per)
                p = owner(chunk, turn)

                @pl.when(p != me)
                def _():
                    out_copy(chunk * per + turn, p, v).start()

                @pl.when(p == me)
                def _():
                    out_own(chunk * per + turn, v).start()
                return carry

            lax.fori_loop(0, per, send, 0)
        return carry

    lax.fori_loop(0, RG, multiply_chunk, 0)

    others(lambda j: piece_out(j).wait_send())
    others(lambda j: window_out(j).wait_send())
    others(lambda j: part_out(j).wait_send())
    w_shift.wait_send()
    for z in range(RG):
        @pl.when(w_target(z) != me)
        def _():
            w_out(z).wait_send()

    def sent(chunk, carry):
        x_copy(chunk).wait_send()
        for i in range(1, RG):
            gather(chunk, ch, rg * CH + along(i) + core, i).wait_send()
            gather(chunk, ch, sibling, RG + i).wait_send()
        gather(chunk, ch, sibling, 0).wait_send()
        return carry

    lax.fori_loop(0, RG, sent, 0)
    for head in range(HK):
        wide_q = pl.ds(head * GROUP * HD, GROUP * HD)
        pltpu.make_async_copy(dq_s.at[:, wide_q], dq_hbm.at[:, wide_q], dq_sem.at[head]).wait()
    for v in range(2):
        others(lambda j: out_copy(0, j, v).wait_send())
        out_own(0, v).wait()
        others(lambda j: remote(outs.at[v, 0], out_part(j, v), os_.at[v, j], or_.at[v, j], ctx=j).wait_recv())


def shards(queries, key_rows, value_rows, out_grad, kv_weight, doc_lengths, block_plan):
    n = lax.axis_size("ctx")
    sections = lax.axis_size("section")
    number = jnp.arange(n, dtype=jnp.int32)
    inverse_plan = jnp.sum(jnp.where(block_plan[None, :] == number[:, None], number[None, :], 0), axis=1, dtype=jnp.int32)
    tokens, width = queries.shape[1:]
    features = kv_weight.shape[1]
    model = features * n
    share = model // CH
    per = n // RG
    smem = pl.BlockSpec(memory_space=pltpu.SMEM)
    vmem = pl.BlockSpec(memory_space=pltpu.VMEM)
    hbm = pl.BlockSpec(memory_space=pl.ANY)
    low = jnp.bfloat16
    dma = pltpu.SemaphoreType.DMA
    query_grad, input_grad = pl.pallas_call(
        functools.partial(kernel, n, sections),
        out_shape=(
            jax.ShapeDtypeStruct((tokens, width), low),
            jax.ShapeDtypeStruct((tokens, model), low),
        ),
        in_specs=[smem, smem, smem, hbm, vmem, vmem, hbm, hbm],
        out_specs=(hbm, hbm),
        scratch_shapes=[
            pltpu.VMEM((tokens, width), low),
            pltpu.VMEM((tokens, width), low),
            pltpu.VMEM((tokens, width), low),
            pltpu.VMEM((CH, SLOTS, BLOCK, HD), low),
            pltpu.VMEM((n, SUB, HD), low),
            pltpu.VMEM((n, BACK, SUB, HD), low),
            pltpu.VMEM((SLOTS * BLOCK, BLOCK), jnp.float32),
            pltpu.VMEM((SLOTS * BLOCK, GROUP * BLOCK), jnp.float32),
            pltpu.VMEM((SLOTS * BLOCK, GROUP * BLOCK), jnp.float32),
            pltpu.VMEM((CH, SLOTS, BLOCK, HD), low),
            pltpu.VMEM((n, SLOTS, SUB, HD), low),
            pltpu.VMEM((n, SUB, HD), low),
            pltpu.VMEM((CH, n, SUB, HD), low),
            pltpu.VMEM((features, CH * HD), low),
            pltpu.VMEM((share, CH * HD), low),
            pltpu.VMEM((2, n, SUB, share // 2), low),
            dma((2,)), dma((HK,)),
            dma((n,)), dma((n,)), dma((n,)), dma((n,)), dma((n,)), dma((n,)),
            dma((RG,)), dma((RG,)), dma((RG, CH)), dma((RG, CH)), dma((2, n)), dma((2, n)),
            dma((5,)), dma, dma, dma((RG,)), dma((RG,)),
        ],
        compiler_params=pltpu.CompilerParams(
            collective_id=0, has_side_effects=True, vmem_limit_bytes=56 * 1024 * 1024
        ),
    )(doc_lengths, block_plan, inverse_plan, queries[0], key_rows[0], value_rows[0], out_grad[0], kv_weight[0])
    return (query_grad[None], input_grad[None])


def solution(mesh):
    spec = P("section", "ctx", None)
    return jax.shard_map(
        shards, mesh=mesh, in_specs=(spec,) * 5 + (P(), P()), out_specs=(spec, spec), check_vma=False
    )
```

```python
import functools
import math

import jax
import jax.numpy as jnp
from jax import lax
from jax.experimental import pallas as pl
from jax.experimental.pallas import tpu as pltpu
from jax.sharding import PartitionSpec as P

HQ = 32
HK = 4
HD = 128
BLOCK = 128
GROUP = HQ // HK
BACK = 8
SLOTS = BACK + 1
CH = 2 * HK
SUB = 32
RG = BLOCK // SUB
MASKED = -1e30
MIX = 13
HALVES = 2
KEYS = 384
MESH = pl.DeviceIdType.MESH


def rem(a, b):
    return lax.rem(a, b)


def div(a, b):
    return lax.div(a, b)


def kernel(
    n, sections, lens, plan, q_hbm, k_ref, v_ref, o_hbm, w_hbm, dq_hbm, out_hbm,
    inv, q_s, o_s, dq_s, kvw, recv1, send2, bias, s_s, g_s, part, recv3, kvo, xbuf, blk, wsh, wfull, outs,
    in_sem, dq_sem, s1s, s1r, s2s, s2r, s3s, s3r, xs, xr, ds_, dr, gs, gr, os_, or_, own_sem, loc_sem, wxs, wxr, wgs, wgr,
):
    me = lax.axis_index("ctx")
    sec = lax.axis_index("section")
    rg = div(me, CH)
    ch = rem(me, CH)
    core = rem(ch, 2)
    column = div(ch, 2)
    before = rem(sec + sections - 1, sections)

    def remote(src, dst, send, recv, **where):
        return pltpu.make_async_remote_copy(
            src_ref=src, dst_ref=dst, send_sem=send, recv_sem=recv,
            device_id=where, device_id_type=MESH,
        )

    def rows(group):
        return pl.ds(pl.multiple_of(group * SUB, SUB), SUB)

    def others(body):
        def step(k, carry):
            body(rem(me + MIX * k, n))
            return carry
        lax.fori_loop(1, n, step, 0)

    load_q = pltpu.make_async_copy(q_hbm, q_s, in_sem.at[0])
    load_o = pltpu.make_async_copy(o_hbm, o_s, in_sem.at[1])
    load_q.start()
    load_o.start()

    barrier = pltpu.get_barrier_semaphore()
    others(lambda j: pl.semaphore_signal(barrier, inc=1, device_id={"ctx": j}, device_id_type=MESH))
    pl.semaphore_signal(barrier, inc=1, device_id={"section": rem(sec + 1, sections)}, device_id_type=MESH)
    for head in range(HK):
        kvw[head, BACK] = k_ref[:, head * HD:(head + 1) * HD]
        kvw[HK + head, BACK] = v_ref[:, head * HD:(head + 1) * HD]

    def invert(b, carry):
        place = jnp.int32(0)
        for p in range(n):
            place = jnp.where(plan[p] == b, p, place)
        inv[b] = place
        return carry

    lax.fori_loop(0, n, invert, 0)
    pl.semaphore_wait(barrier, n)

    def piece_out(j):
        return remote(kvw.at[rem(j, CH), BACK, rows(div(j, CH))], recv1.at[me], s1s.at[j], s1r.at[me], ctx=j)

    others(lambda j: piece_out(j).start())
    w_shift = remote(w_hbm, wsh, wxs, wxr, section=before)
    w_shift.start()
    recv1[me] = kvw[ch, BACK, rows(rg)]

    token_block = plan[me]
    row_token = token_block * BLOCK + lax.broadcasted_iota(jnp.int32, (1, BLOCK), 1)
    start = jnp.zeros((1, BLOCK), jnp.int32)
    end = jnp.int32(0)
    for j in range(lens.shape[0]):
        end = end + lens[j]
        start = jnp.where(row_token >= end, end, start)
    key_token = (token_block - BACK) * BLOCK + lax.broadcasted_iota(jnp.int32, (SLOTS * BLOCK, BLOCK), 0)
    seen = jnp.logical_and(key_token >= start, key_token <= row_token)
    bias[...] = jnp.where(seen, 0.0, MASKED)

    def piece_in(j):
        return remote(kvw.at[0, BACK, rows(0)], recv1.at[j], s1s.at[j], s1r.at[j], ctx=j)

    others(lambda j: piece_in(j).wait_recv())

    def window_out(d):
        return remote(send2.at[d], kvw.at[ch, pl.ds(0, BACK), rows(rg)], s2s.at[d], s2r.at[me], ctx=d)

    head_of = rem(ch, HK)

    def window_own():
        return pltpu.make_async_copy(send2.at[me], kvw.at[ch, pl.ds(0, BACK), rows(rg)], loc_sem.at[0])

    def window_step(i, carry):
        d = HK * rem(div(me, HK) + 3 * i, n // HK) + rem(head_of - div(i, n // HK) + HK, HK)
        first = plan[d] - BACK
        for w in range(BACK):
            send2[d, w] = recv1[inv[jnp.maximum(first + w, 0)]]

        @pl.when(d != me)
        def _():
            window_out(d).start()

        @pl.when(d == me)
        def _():
            window_own().start()
        return carry

    lax.fori_loop(0, n, window_step, 0)

    def window_in(j):
        return remote(send2.at[j], kvw.at[rem(j, CH), pl.ds(0, BACK), rows(div(j, CH))], s2s.at[j], s2r.at[j], ctx=j)

    place = rg * (1 - core) + column * core
    w_slot = 2 * core + rem(place, 2)
    shard = w_hbm.shape[0]

    def device(z, y, core):
        return z * CH + 2 * y + core

    def w_rows(slot):
        return wfull.at[pl.ds(pl.multiple_of(slot * shard, shard), shard)]

    def w_target(i):
        return device(i * (1 - core) + rg * core, column * (1 - core) + i * core, div(place, 2))

    def w_source(u):
        if u < 2:
            return device(2 * core + u, column, 0)
        return device(rg, 2 * core + u - 2, 1)

    def w_out(i):
        return remote(wsh, w_rows(w_slot), wgs.at[i], wgr.at[w_slot], ctx=w_target(i))

    def w_own():
        return pltpu.make_async_copy(wsh, w_rows(w_slot), loc_sem.at[1])

    def spread_weights():
        w_shift.wait_recv()
        for z in range(RG):
            @pl.when(w_target(z) != me)
            def _():
                w_out(z).start()

            @pl.when(w_target(z) == me)
            def _():
                w_own().start()

    load_q.wait()
    load_o.wait()

    scale = 1.0 / math.sqrt(HD)
    power = scale * math.log2(math.e)
    nt = (((1,), (1,)), ((), ()))
    tn = (((0,), (0,)), ((), ()))

    def part_out(j):
        return remote(part.at[rem(j, CH), :, rows(div(j, CH))], recv3.at[me], s3s.at[j], s3r.at[me], ctx=j)

    def part_own():
        return pltpu.make_async_copy(part.at[ch, :, rows(rg)], recv3.at[me], loc_sem.at[2])

    def one_head(step, carry):
        head = rem(step + me, HK)

        def arrived(i, carry):
            j = HK * i + head

            @pl.when(j != me)
            def _():
                window_in(j).wait_recv()

            @pl.when(j == me)
            def _():
                window_own().wait()
            return carry

        lax.fori_loop(0, n // HK, arrived, 0)

        def columns(i):
            return pl.ds(pl.multiple_of((head * GROUP + i) * HD, HD), HD)

        q2 = jnp.concatenate([q_s[:, columns(i)] for i in range(GROUP)], axis=0)
        o2 = jnp.concatenate([o_s[:, columns(i)] for i in range(GROUP)], axis=0)
        wide = GROUP * BLOCK
        spans = [(slice(i, i + KEYS), slice(i // BLOCK, (i + KEYS) // BLOCK)) for i in range(0, SLOTS * BLOCK, KEYS)]

        def folded(x, over):
            return over(x.reshape(KEYS // 8, 8, wide), axis=0)

        peak = None
        for span, slots in spans:
            b = bias[span]
            keys = kvw[head, slots].reshape(KEYS, HD)
            scores = lax.dot_general(keys, q2, nt, preferred_element_type=jnp.float32)
            scores = scores + jnp.concatenate([b] * GROUP, axis=1)
            s_s[span] = scores
            top = folded(scores, jnp.max)
            peak = top if peak is None else jnp.maximum(peak, top)
            values = kvw[HK + head, slots].reshape(KEYS, HD)
            g_s[span] = lax.dot_general(values, o2, nt, preferred_element_type=jnp.float32)
        peak = jnp.max(peak, axis=0, keepdims=True)
        total = jnp.zeros((8, wide), jnp.float32)
        weighted = jnp.zeros((8, wide), jnp.float32)
        for span, slots in spans:
            terms = jnp.exp2((s_s[span] - peak) * power)
            s_s[span] = terms
            total = total + folded(terms, jnp.sum)
            weighted = weighted + folded(terms * g_s[span], jnp.sum)
        inverse = 1.0 / jnp.sum(total, axis=0, keepdims=True)
        delta = jnp.sum(weighted, axis=0, keepdims=True) * inverse
        dq = jnp.zeros((wide, HD), jnp.float32)
        for span, slots in spans:
            prob = s_s[span] * inverse
            prob_low = prob.astype(jnp.bfloat16)
            score_low = (prob * (g_s[span] - delta)).astype(jnp.bfloat16)
            dv = jnp.dot(prob_low, o2, preferred_element_type=jnp.float32)
            dk = jnp.dot(score_low, q2, preferred_element_type=jnp.float32) * scale
            part[HK + head, slots] = dv.astype(jnp.bfloat16).reshape(KEYS // BLOCK, BLOCK, HD)
            part[head, slots] = dk.astype(jnp.bfloat16).reshape(KEYS // BLOCK, BLOCK, HD)
            keys = kvw[head, slots].reshape(KEYS, HD)
            dq = dq + lax.dot_general(score_low, keys, tn, preferred_element_type=jnp.float32)
        for i in range(GROUP):
            dq_s[:, columns(i)] = (dq[i * BLOCK:(i + 1) * BLOCK] * scale).astype(jnp.bfloat16)

        def send(i, carry):
            turn = rem(3 * i + div(me, HK), n // HK)
            j = turn * HK + head

            @pl.when(j != me)
            def _():
                part_out(j).start()

            @pl.when(j == me)
            def _():
                part_own().start()
            return carry

        lax.fori_loop(0, 2 * RG, send, 0)
        wide = pl.ds(pl.multiple_of(head * GROUP * HD, GROUP * HD), GROUP * HD)
        pltpu.make_async_copy(dq_s.at[:, wide], dq_hbm.at[:, wide], dq_sem.at[head]).start()
        return carry

    lax.fori_loop(0, HK, one_head, 0)

    def part_in(j):
        return remote(part.at[0, :, rows(0)], recv3.at[j], s3s.at[j], s3r.at[j], ctx=j)

    others(lambda j: part_in(j).wait_recv())
    part_own().wait()
    spread_weights()

    per = n // RG

    def owner(chunk, i):
        z = div(i, 2)
        return z * CH + 2 * rem(chunk - z + RG, RG) + rem(i, 2)

    def blocks(chunk):
        return pl.ds(pl.multiple_of(chunk * per, per), per)

    def x_copy(chunk):
        return remote(kvo.at[blocks(chunk)], xbuf.at[blocks(chunk)], xs.at[chunk], xr.at[chunk], section=before)

    def reduce_chunk(step, carry):
        chunk = rem(step + rg, RG)

        def one_block(i, carry):
            p = owner(chunk, i)
            total = jnp.zeros((SUB, HD), jnp.float32)
            for w in range(SLOTS):
                later = plan[p] + BACK - w
                term = recv3[inv[jnp.minimum(later, n - 1)], w].astype(jnp.float32)
                total = total + jnp.where(later < n, term, 0.0)
            kvo[chunk * per + i] = total.astype(jnp.bfloat16)
            return carry

        lax.fori_loop(0, per, one_block, 0)
        x_copy(chunk).start()
        return carry

    lax.fori_loop(0, RG, reduce_chunk, 0)

    def deliver(index, p):
        return remote(xbuf.at[index], blk.at[0, 0, ch, rows(rg)], ds_.at[p], dr.at[me], ctx=p)

    def deliver_own(index):
        return pltpu.make_async_copy(xbuf.at[index], blk.at[0, 0, ch, rows(rg)], loc_sem.at[3])

    def deliver_chunk(step, carry):
        chunk = rem(step + rg, RG)
        x_copy(chunk).wait_recv()

        def one(i, carry):
            turn = rem(3 * i + ch, per)
            p = owner(chunk, turn)

            @pl.when(p != me)
            def _():
                deliver(chunk * per + turn, p).start()

            @pl.when(p == me)
            def _():
                deliver_own(chunk * per + turn).start()
            return carry

        lax.fori_loop(0, per, one, 0)
        return carry

    lax.fori_loop(0, RG, deliver_chunk, 0)

    def delivered(j):
        return remote(xbuf.at[0], blk.at[0, 0, rem(j, CH), rows(div(j, CH))], ds_.at[j], dr.at[j], ctx=j)

    others(lambda j: delivered(j).wait_recv())
    deliver_own(0).wait()

    sibling = device(rg, column, 1 - core)
    half = BLOCK // HALVES

    def half_rows(q):
        return pl.ds(pl.multiple_of(q * half, half), half)

    def chip(axis, i, core):
        return device(rem(rg + axis * i, RG), rem(column + (1 - axis) * i, RG), core)

    def along(q, axis, i):
        return remote(
            blk.at[0, 0, :, half_rows(q)], blk.at[3 * axis + RG - i, 0, :, half_rows(q)],
            gs.at[q, 3 * axis + i], gr.at[q, 3 * axis + RG - i, 0], ctx=chip(axis, i, core),
        )

    def across(q, spot):
        return remote(
            blk.at[spot, 0, :, half_rows(q)], blk.at[spot, 1, :, half_rows(q)],
            gs.at[q, 7 + spot], gr.at[q, spot, 1], ctx=sibling,
        )

    def arrival(q, spot, other):
        return remote(
            blk.at[spot, other, :, half_rows(q)], blk.at[spot, other, :, half_rows(q)],
            gs.at[q, 0], gr.at[q, spot, other], ctx=sibling,
        )

    def far(t):
        return t + (t // 2) * (5 - 2 * t)

    for q in range(HALVES):
        for t in range(1, RG):
            for axis in range(2):
                along(q, axis, far(t)).start()
        across(q, 0).start()

    for u in range(RG):
        @pl.when(w_source(u) != me)
        def _():
            remote(wsh, w_rows(u), wgs.at[u], wgr.at[u], ctx=w_source(u)).wait_recv()

        @pl.when(w_source(u) == me)
        def _():
            w_own().wait()

    def out_part(j, axis, v, q):
        z, y, b = div(j, CH), rem(div(j, 2), RG), rem(j, 2)
        number = (1 - axis) * device(2 * b + v, y, 0) + axis * device(z, 2 * b + v, 1)
        return out_hbm.at[half_rows(q), pl.ds(pl.multiple_of(number * shard, shard), shard)]

    def out_copy(q, axis, i, other, v):
        core_there = core + other * (1 - 2 * core)
        return remote(
            outs.at[q, axis, i, other, v], out_part(me, axis, v, q),
            os_.at[q, axis, i, other, v], or_.at[q, axis, rem(RG - i, RG), other, v], ctx=chip(axis, i, core_there),
        )

    def out_own(q, axis, v):
        return pltpu.make_async_copy(outs.at[q, axis, 0, 0, v], out_part(me, axis, v, q), own_sem.at[q, axis, v])

    def multiply(q):
        def one(m, carry):
            axis, t = rem(m, 2), div(m, 2)
            i = t + div(t, 2) * (5 - 2 * t)
            spot = jnp.where(i == 0, 0, 3 * axis + i)

            @pl.when(m != 1)
            def _():
                arrival(q, spot, 1).wait_recv()

            left = jnp.concatenate(
                [
                    jnp.concatenate([blk[spot, other, c, q * half:(q + 1) * half] for c in range(CH)], axis=1)
                    for other in range(2)
                ],
                axis=0,
            )
            right = wfull[pl.ds(pl.multiple_of(axis * 2 * shard, 2 * shard), 2 * shard)]
            product = lax.dot_general(left, right, nt, preferred_element_type=jnp.float32).astype(jnp.bfloat16)
            for other in range(2):
                for v in range(2):
                    outs[q, axis, i, other, v] = product[other * half:(other + 1) * half, v * shard:(v + 1) * shard]
            for v in range(2):
                out_copy(q, axis, i, 1, v).start()

                @pl.when(i != 0)
                def _():
                    out_copy(q, axis, i, 0, v).start()

                @pl.when(i == 0)
                def _():
                    out_own(q, axis, v).start()
            return carry

        lax.fori_loop(0, 2 * RG, one, 0)

    for q in range(HALVES):
        def share(m, carry):
            axis, t = rem(m, 2), div(m, 2)
            spot = 3 * axis + t + div(t, 2) * (5 - 2 * t)
            arrival(q, spot, 0).wait_recv()
            across(q, spot).start()
            return carry

        lax.fori_loop(2, 2 * RG, share, 0)
        multiply(q)

    others(lambda j: piece_out(j).wait_send())
    others(lambda j: window_out(j).wait_send())
    others(lambda j: part_out(j).wait_send())
    w_shift.wait_send()
    for z in range(RG):
        @pl.when(w_target(z) != me)
        def _():
            w_out(z).wait_send()

        x_copy(z).wait_send()

    others(lambda j: deliver(0, j).wait_send())
    for q in range(HALVES):
        for axis in range(2):
            for i in range(1, RG):
                along(q, axis, i).wait_send()
                across(q, 3 * axis + i).wait_send()
        across(q, 0).wait_send()
    for head in range(HK):
        wide_q = pl.ds(head * GROUP * HD, GROUP * HD)
        pltpu.make_async_copy(dq_s.at[:, wide_q], dq_hbm.at[:, wide_q], dq_sem.at[head]).wait()

    def finish(m, carry):
        axis, i = div(m, RG), rem(m, RG)
        for q in range(HALVES):
            for v in range(2):
                for other in range(2):
                    there = core + other * (1 - 2 * core)
                    incoming = remote(
                        outs.at[q, axis, i, other, v], out_part(chip(axis, i, there), axis, v, q),
                        os_.at[q, axis, i, other, v], or_.at[q, axis, i, other, v], ctx=sibling,
                    )

                    @pl.when(i + other > 0)
                    def _():
                        out_copy(q, axis, i, other, v).wait_send()
                        incoming.wait_recv()

                @pl.when(i == 0)
                def _():
                    out_own(q, axis, v).wait()
        return carry

    lax.fori_loop(0, 2 * RG, finish, 0)


def shards(queries, key_rows, value_rows, out_grad, kv_weight, doc_lengths, block_plan):
    n = lax.axis_size("ctx")
    sections = lax.axis_size("section")
    tokens, width = queries.shape[1:]
    features = kv_weight.shape[1]
    model = features * n
    share = model // CH
    smem = pl.BlockSpec(memory_space=pltpu.SMEM)
    vmem = pl.BlockSpec(memory_space=pltpu.VMEM)
    hbm = pl.BlockSpec(memory_space=pl.ANY)
    low = jnp.bfloat16
    dma = pltpu.SemaphoreType.DMA
    query_grad, input_grad = pl.pallas_call(
        functools.partial(kernel, n, sections),
        out_shape=(
            jax.ShapeDtypeStruct((tokens, width), low),
            jax.ShapeDtypeStruct((tokens, model), low),
        ),
        in_specs=[smem, smem, hbm, vmem, vmem, hbm, hbm],
        out_specs=(hbm, hbm),
        scratch_shapes=[
            pltpu.SMEM((n,), jnp.int32),
            pltpu.VMEM((tokens, width), low),
            pltpu.VMEM((tokens, width), low),
            pltpu.VMEM((tokens, width), low),
            pltpu.VMEM((CH, SLOTS, BLOCK, HD), low),
            pltpu.VMEM((n, SUB, HD), low),
            pltpu.VMEM((n, BACK, SUB, HD), low),
            pltpu.VMEM((SLOTS * BLOCK, BLOCK), jnp.float32),
            pltpu.VMEM((SLOTS * BLOCK, GROUP * BLOCK), jnp.float32),
            pltpu.VMEM((SLOTS * BLOCK, GROUP * BLOCK), jnp.float32),
            pltpu.VMEM((CH, SLOTS, BLOCK, HD), low),
            pltpu.VMEM((n, SLOTS, SUB, HD), low),
            pltpu.VMEM((n, SUB, HD), low),
            pltpu.VMEM((n, SUB, HD), low),
            pltpu.VMEM((7, 2, CH, BLOCK, HD), low),
            pltpu.VMEM((features, CH * HD), low),
            pltpu.VMEM((share, CH * HD), low),
            pltpu.VMEM((HALVES, 2, RG, 2, 2, BLOCK // HALVES, features), low),
            dma((2,)), dma((HK,)),
            dma((n,)), dma((n,)), dma((n,)), dma((n,)), dma((n,)), dma((n,)),
            dma((RG,)), dma((RG,)), dma((n,)), dma((n,)), dma((HALVES, 14)), dma((HALVES, 7, 2)),
            dma((HALVES, 2, RG, 2, 2)), dma((HALVES, 2, RG, 2, 2)), dma((HALVES, 2, 2)),
            dma((4,)), dma, dma, dma((RG,)), dma((RG,)),
        ],
        compiler_params=pltpu.CompilerParams(
            collective_id=0, has_side_effects=True, vmem_limit_bytes=56 * 1024 * 1024
        ),
    )(doc_lengths, block_plan, queries[0], key_rows[0], value_rows[0], out_grad[0], kv_weight[0])
    return (query_grad[None], input_grad[None])


def solution(mesh):
    spec = P("section", "ctx", None)
    return jax.shard_map(
        shards, mesh=mesh, in_specs=(spec,) * 5 + (P(), P()), out_specs=(spec, spec), check_vma=False
    )
```

```python
import functools
import math

import jax
import jax.numpy as jnp
from jax import lax
from jax.experimental import pallas as pl
from jax.experimental.pallas import tpu as pltpu
from jax.sharding import PartitionSpec as P

HQ = 32
HK = 4
HD = 128
BLOCK = 128
GROUP = HQ // HK
BACK = 8
SLOTS = BACK + 1
CH = 2 * HK
SUB = 32
RG = BLOCK // SUB
MASKED = -1e30
MIX = 13
HALVES = 2
KEYS = 384
MESH = pl.DeviceIdType.MESH


def rem(a, b):
    return lax.rem(a, b)


def div(a, b):
    return lax.div(a, b)


def kernel(
    n, sections, lens_hbm, plan_hbm, q_hbm, k_hbm, v_hbm, o_hbm, w_hbm, dq_hbm, out_hbm,
    lens, plan, inv, q_s, o_s, dq_s, kvw, hold, send2, bias, s_s, g_s, part, terms, sums, totals, kvo, xbuf, blk, wsh, wfull, outs,
    in_sem, kv_sem, dq_sem, s1s, s1r, g1s, g1r, s2s, s2r, s3s, s3r, rs, rr, xs, xr, ds_, dr, gs, gr, os_, or_, own_sem, loc_sem, wxs, wxr, wgs, wgr,
):
    me = lax.axis_index("ctx")
    sec = lax.axis_index("section")
    rg = div(me, CH)
    ch = rem(me, CH)
    core = rem(ch, 2)
    column = div(ch, 2)
    before = rem(sec + sections - 1, sections)

    def remote(src, dst, send, recv, **where):
        return pltpu.make_async_remote_copy(
            src_ref=src, dst_ref=dst, send_sem=send, recv_sem=recv,
            device_id=where, device_id_type=MESH,
        )

    load_lens = pltpu.make_async_copy(lens_hbm, lens, in_sem.at[2])
    load_plan = pltpu.make_async_copy(plan_hbm, plan, in_sem.at[3])
    load_q = pltpu.make_async_copy(q_hbm, q_s, in_sem.at[0])
    load_o = pltpu.make_async_copy(o_hbm, o_s, in_sem.at[1])
    load_kv = [
        pltpu.make_async_copy(
            (v_hbm if kind else k_hbm).at[:, pl.ds(head * HD, HD)], kvw.at[kind * HK + head, BACK], kv_sem.at[kind, head]
        )
        for kind in range(2)
        for head in range(HK)
    ]
    for load in (load_plan, load_lens, *load_kv, load_q, load_o):
        load.start()

    def device(z, y, core):
        return z * CH + 2 * y + core

    halves = BLOCK // 2
    line = (2 * column + core, 2 * rg + core)

    def mate(kind, m):
        return device(rg, div(m, 2), rem(m, 2)) if kind == 0 else device(div(m, 2), column, rem(m, 2))

    barrier = pltpu.get_barrier_semaphore()

    def greet(j):
        pl.semaphore_signal(barrier, inc=1, device_id={"ctx": j}, device_id_type=MESH)

    for k in range(1, CH):
        greet(mate(0, rem(line[0] + k, CH)))
    for k in range(1, RG):
        for there in range(2):
            greet(device(rem(rg + k, RG), column, there))
    pl.semaphore_signal(barrier, inc=1, device_id={"section": rem(sec + 1, sections)}, device_id_type=MESH)
    load_plan.wait()
    load_lens.wait()

    def invert(b, carry):
        place = jnp.int32(0)
        for p in range(n):
            place = jnp.where(plan[p] == b, p, place)
        inv[0, b] = place
        inv[1, b] = rem(div(place, 2), RG) * CH + div(place, CH) * 2 + rem(place, 2)
        return carry

    lax.fori_loop(0, n, invert, 0)
    for load in load_kv:
        load.wait()
    pl.semaphore_wait(barrier, CH - 1 + 2 * (RG - 1) + 1)

    def held_head(m):
        return rem(div(m, 2) + 2 * rem(m, 2), HK)

    def half_of(m):
        return pl.ds(pl.multiple_of(rem(m, 2) * halves, halves), halves)

    held = (me, column * CH + 2 * rg + core)

    def piece_out(kind, m):
        return remote(
            kvw.at[kind * HK + held_head(m), BACK, half_of(m)], hold.at[kind, held[kind]],
            s1s.at[kind, m], s1r.at[kind, line[kind]], ctx=mate(kind, m),
        )

    def piece_in(kind, m):
        return remote(
            kvw.at[0, BACK, half_of(0)], hold.at[kind, m if kind else rg * CH + m],
            s1s.at[kind, m], s1r.at[kind, m], ctx=mate(kind, m),
        )

    def mates(body):
        for k in range(1, CH):
            for kind in range(2):
                body(kind, rem(line[kind] + 3 * k, CH))

    mates(lambda kind, m: piece_out(kind, m).start())
    w_shift = remote(w_hbm, wsh, wxs, wxr, section=before)
    w_shift.start()
    for kind in range(2):
        hold[kind, held[kind]] = kvw[kind * HK + held_head(line[kind]), BACK, half_of(line[kind])]

    token_block = plan[me]
    row_token = token_block * BLOCK + lax.broadcasted_iota(jnp.int32, (1, BLOCK), 1)
    start = jnp.zeros((1, BLOCK), jnp.int32)
    end = jnp.int32(0)
    for j in range(lens.shape[0]):
        end = end + lens[j]
        start = jnp.where(row_token >= end, end, start)
    key_token = (token_block - BACK) * BLOCK + lax.broadcasted_iota(jnp.int32, (SLOTS * BLOCK, BLOCK), 0)
    seen = jnp.logical_and(key_token >= start, key_token <= row_token)
    bias[...] = jnp.where(seen, 0.0, MASKED)
    for kind in range(2):
        terms[kind, CH] = jnp.zeros((SLOTS, halves, HD), jnp.bfloat16)

    def group(kind, i):
        across_lines = rg if kind == 0 else column
        return hold.at[kind, pl.ds(pl.multiple_of(rem(across_lines + i, RG) * CH, CH), CH)]

    def peer(kind, i):
        return device(rem(rg + i, RG), column, core) if kind == 0 else device(rg, rem(column + i, RG), core)

    def group_out(kind, i):
        return remote(group(kind, 0), group(kind, 0), g1s.at[kind, i], g1r.at[kind, RG - i], ctx=peer(kind, i))

    def group_in(kind, i):
        return remote(group(kind, i), group(kind, i), g1s.at[kind, i], g1r.at[kind, i], ctx=peer(kind, i))

    mates(lambda kind, m: piece_in(kind, m).wait_recv())
    for i in (1, 3, 2):
        for kind in range(2):
            group_out(kind, i).start()
    for i in (1, 3, 2):
        for kind in range(2):
            group_in(kind, i).wait_recv()

    def window_slots(kind, m):
        return kvw.at[kind * HK + held_head(m), pl.ds(0, BACK), half_of(m)]

    def window_out(kind, m):
        return remote(
            send2.at[kind, m], window_slots(kind, line[kind]), s2s.at[kind, m], s2r.at[kind, line[kind]], ctx=mate(kind, m)
        )

    def window_own(kind):
        return pltpu.make_async_copy(send2.at[kind, line[kind]], window_slots(kind, line[kind]), loc_sem.at[4 * kind])

    def window_in(kind, m):
        return remote(send2.at[kind, m], window_slots(kind, m), s2s.at[kind, m], s2r.at[kind, m], ctx=mate(kind, m))

    turn_of = rem(rg + column, HK)

    def window_step(i, carry):
        for kind in range(2):
            start_at = held_head(line[kind]) + 2 * RG - div(i, 2) - (rg if kind == 0 else column)
            m = 2 * rem(start_at, RG) + rem(i, 2)
            first = plan[mate(kind, m)] - BACK
            for w in range(BACK):
                send2[kind, m, w] = hold[kind, inv[kind, jnp.maximum(first + w, 0)]]

            @pl.when(m != line[kind])
            def _():
                window_out(kind, m).start()

            @pl.when(m == line[kind])
            def _():
                window_own(kind).start()
        return carry

    lax.fori_loop(0, CH, window_step, 0)

    place = rg * (1 - core) + column * core
    w_slot = 2 * core + rem(place, 2)
    shard = w_hbm.shape[0]

    def w_rows(slot):
        return wfull.at[pl.ds(pl.multiple_of(slot * shard, shard), shard)]

    def w_target(i):
        return device(i * (1 - core) + rg * core, column * (1 - core) + i * core, div(place, 2))

    def w_source(u):
        if u < 2:
            return device(2 * core + u, column, 0)
        return device(rg, 2 * core + u - 2, 1)

    def w_out(i):
        return remote(wsh, w_rows(w_slot), wgs.at[i], wgr.at[w_slot], ctx=w_target(i))

    def w_own():
        return pltpu.make_async_copy(wsh, w_rows(w_slot), loc_sem.at[1])

    def spread_weights():
        w_shift.wait_recv()
        for z in range(RG):
            @pl.when(w_target(z) != me)
            def _():
                w_out(z).start()

            @pl.when(w_target(z) == me)
            def _():
                w_own().start()

    load_q.wait()
    load_o.wait()

    scale = 1.0 / math.sqrt(HD)
    power = scale * math.log2(math.e)
    nt = (((1,), (1,)), ((), ()))
    tn = (((0,), (0,)), ((), ()))

    def term_out(kind, m):
        return remote(
            part.at[kind * HK + held_head(m), :, half_of(m)], terms.at[kind, line[kind]],
            s3s.at[kind, m], s3r.at[kind, line[kind]], ctx=mate(kind, m),
        )

    def term_own(kind):
        m = line[kind]
        return pltpu.make_async_copy(part.at[kind * HK + held_head(m), :, half_of(m)], terms.at[kind, m], loc_sem.at[2 + 3 * kind])

    def term_in(kind, m):
        return remote(
            part.at[0, :, half_of(0)], terms.at[kind, m], s3s.at[kind, m], s3r.at[kind, m], ctx=mate(kind, m)
        )

    def one_head(step, carry):
        head = rem(step + turn_of, HK)
        for half in range(2):
            m = 2 * rem(head + RG - 2 * half, RG) + half
            for kind in range(2):
                @pl.when(m != line[kind])
                def _():
                    window_in(kind, m).wait_recv()

                @pl.when(m == line[kind])
                def _():
                    window_own(kind).wait()

        @pl.when(step == 1)
        def _():
            spread_weights()

        def columns(i):
            return pl.ds(pl.multiple_of((head * GROUP + i) * HD, HD), HD)

        q2 = jnp.concatenate([q_s[:, columns(i)] for i in range(GROUP)], axis=0)
        o2 = jnp.concatenate([o_s[:, columns(i)] for i in range(GROUP)], axis=0)
        wide = GROUP * BLOCK
        spans = [(slice(i, i + KEYS), slice(i // BLOCK, (i + KEYS) // BLOCK)) for i in range(0, SLOTS * BLOCK, KEYS)]

        def folded(x, over):
            return over(x.reshape(KEYS // 8, 8, wide), axis=0)

        peak = None
        for span, slots in spans:
            b = bias[span]
            keys = kvw[head, slots].reshape(KEYS, HD)
            scores = lax.dot_general(keys, q2, nt, preferred_element_type=jnp.float32)
            scores = scores + jnp.concatenate([b] * GROUP, axis=1)
            s_s[span] = scores
            top = folded(scores, jnp.max)
            peak = top if peak is None else jnp.maximum(peak, top)
            values = kvw[HK + head, slots].reshape(KEYS, HD)
            g_s[span] = lax.dot_general(values, o2, nt, preferred_element_type=jnp.float32)
        peak = jnp.max(peak, axis=0, keepdims=True)
        total = jnp.zeros((8, wide), jnp.float32)
        weighted = jnp.zeros((8, wide), jnp.float32)
        for span, slots in spans:
            terms = jnp.exp2((s_s[span] - peak) * power)
            s_s[span] = terms
            total = total + folded(terms, jnp.sum)
            weighted = weighted + folded(terms * g_s[span], jnp.sum)
        inverse = 1.0 / jnp.sum(total, axis=0, keepdims=True)
        delta = jnp.sum(weighted, axis=0, keepdims=True) * inverse
        dq = jnp.zeros((wide, HD), jnp.float32)
        for span, slots in spans:
            prob = s_s[span] * inverse
            prob_low = prob.astype(jnp.bfloat16)
            score_low = (prob * (g_s[span] - delta)).astype(jnp.bfloat16)
            dv = jnp.dot(prob_low, o2, preferred_element_type=jnp.float32)
            dk = jnp.dot(score_low, q2, preferred_element_type=jnp.float32) * scale
            part[HK + head, slots] = dv.astype(jnp.bfloat16).reshape(KEYS // BLOCK, BLOCK, HD)
            part[head, slots] = dk.astype(jnp.bfloat16).reshape(KEYS // BLOCK, BLOCK, HD)
            keys = kvw[head, slots].reshape(KEYS, HD)
            dq = dq + lax.dot_general(score_low, keys, tn, preferred_element_type=jnp.float32)
        for i in range(GROUP):
            dq_s[:, columns(i)] = (dq[i * BLOCK:(i + 1) * BLOCK] * scale).astype(jnp.bfloat16)

        for half in range(2):
            m = 2 * rem(head + RG - 2 * half, RG) + half
            for kind in range(2):
                @pl.when(m != line[kind])
                def _():
                    term_out(kind, m).start()

                @pl.when(m == line[kind])
                def _():
                    term_own(kind).start()

        wide = pl.ds(pl.multiple_of(head * GROUP * HD, GROUP * HD), GROUP * HD)
        pltpu.make_async_copy(dq_s.at[:, wide], dq_hbm.at[:, wide], dq_sem.at[head]).start()
        return carry

    lax.fori_loop(0, HK, one_head, 0)

    mates(lambda kind, m: term_in(kind, m).wait_recv())
    for kind in range(2):
        term_own(kind).wait()

    def total_out(kind, i):
        to = rem((rg if kind == 0 else column) + i, RG)
        return remote(
            sums.at[kind, pl.ds(pl.multiple_of(to * CH, CH), CH)], totals.at[kind, RG - i],
            rs.at[kind, i], rr.at[kind, RG - i], ctx=peer(kind, i),
        )

    def total_in(kind, i):
        return remote(
            sums.at[kind, pl.ds(0, CH)], totals.at[kind, i], rs.at[kind, i], rr.at[kind, i], ctx=peer(kind, i)
        )

    for i in (1, 2, 3, 0):
        for kind in range(2):
            here = rg if kind == 0 else column
            to = rem(here + i, RG)

            def one_block(e, carry):
                p = device(to, div(e, 2), rem(e, 2)) if kind == 0 else device(div(e, 2), to, rem(e, 2))
                total = jnp.zeros((halves, HD), jnp.float32)
                for w in range(SLOTS):
                    later = plan[p] + BACK - w
                    source = inv[kind, jnp.minimum(later, n - 1)]
                    wanted = jnp.logical_and(later < n, div(source, CH) == here)
                    total = total + terms[kind, jnp.where(wanted, rem(source, CH), CH), w].astype(jnp.float32)
                sums[kind, to * CH + e] = total.astype(jnp.bfloat16)
                return carry

            lax.fori_loop(0, CH, one_block, 0)
            if i > 0:
                total_out(kind, i).start()

    def x_copy(kind):
        return remote(kvo.at[kind], xbuf.at[kind], xs.at[kind], xr.at[kind], section=before)

    for kind in range(2):
        here = rg if kind == 0 else column
        for i in range(1, RG):
            total_in(kind, i).wait_recv()

        def one_sum(e, carry):
            total = sums[kind, here * CH + e].astype(jnp.float32)
            for i in range(1, RG):
                total = total + totals[kind, i, e].astype(jnp.float32)
            kvo[kind, e] = total.astype(jnp.bfloat16)
            return carry

        lax.fori_loop(0, CH, one_sum, 0)
        x_copy(kind).start()

    def owned(kind, m):
        return blk.at[0, 0, kind * HK + held_head(m), half_of(m)]

    def deliver(kind, m):
        return remote(
            xbuf.at[kind, m], owned(kind, line[kind]), ds_.at[kind, m], dr.at[kind, line[kind]], ctx=mate(kind, m)
        )

    def deliver_own(kind):
        return pltpu.make_async_copy(xbuf.at[kind, line[kind]], owned(kind, line[kind]), loc_sem.at[3 + 3 * kind])

    def delivered(kind, m):
        return remote(xbuf.at[kind, m], owned(kind, m), ds_.at[kind, m], dr.at[kind, m], ctx=mate(kind, m))

    for kind in range(2):
        x_copy(kind).wait_recv()
        for k in range(1, CH):
            deliver(kind, rem(line[kind] + 3 * k, CH)).start()
        deliver_own(kind).start()

    mates(lambda kind, m: delivered(kind, m).wait_recv())
    for kind in range(2):
        deliver_own(kind).wait()

    sibling = device(rg, column, 1 - core)
    half = BLOCK // HALVES

    def half_rows(q):
        return pl.ds(pl.multiple_of(q * half, half), half)

    def chip(axis, i, core):
        return device(rem(rg + axis * i, RG), rem(column + (1 - axis) * i, RG), core)

    def along(q, axis, i):
        return remote(
            blk.at[0, 0, :, half_rows(q)], blk.at[3 * axis + RG - i, 0, :, half_rows(q)],
            gs.at[q, 3 * axis + i], gr.at[q, 3 * axis + RG - i, 0], ctx=chip(axis, i, core),
        )

    def across(q, spot):
        return remote(
            blk.at[spot, 0, :, half_rows(q)], blk.at[spot, 1, :, half_rows(q)],
            gs.at[q, 7 + spot], gr.at[q, spot, 1], ctx=sibling,
        )

    def arrival(q, spot, other):
        return remote(
            blk.at[spot, other, :, half_rows(q)], blk.at[spot, other, :, half_rows(q)],
            gs.at[q, 0], gr.at[q, spot, other], ctx=sibling,
        )

    ways = ((1, 3), (3, 1))

    def onward(q, axis):
        to, source = ways[q]
        return remote(
            blk.at[3 * axis + source, 0, :, half_rows(q)], blk.at[3 * axis + 2, 0, :, half_rows(q)],
            gs.at[q, 3 * axis + 2], gr.at[q, 3 * axis + 2, 0], ctx=chip(axis, to, core),
        )

    for q in range(HALVES):
        for k in range(2):
            for axis in range(2):
                along(q, axis, ways[q][k]).start()
        across(q, 0).start()

    for u in range(RG):
        @pl.when(w_source(u) != me)
        def _():
            remote(wsh, w_rows(u), wgs.at[u], wgr.at[u], ctx=w_source(u)).wait_recv()

        @pl.when(w_source(u) == me)
        def _():
            w_own().wait()

    def out_part(j, axis, v, q):
        z, y, b = div(j, CH), rem(div(j, 2), RG), rem(j, 2)
        number = (1 - axis) * device(2 * b + v, y, 0) + axis * device(z, 2 * b + v, 1)
        return out_hbm.at[half_rows(q), pl.ds(pl.multiple_of(number * shard, shard), shard)]

    def out_copy(q, axis, i, other, v):
        core_there = core + other * (1 - 2 * core)
        return remote(
            outs.at[q, axis, i, other, v], out_part(me, axis, v, q),
            os_.at[q, axis, i, other, v], or_.at[q, axis, rem(RG - i, RG), other, v], ctx=chip(axis, i, core_there),
        )

    def out_own(q, axis, v):
        return pltpu.make_async_copy(outs.at[q, axis, 0, 0, v], out_part(me, axis, v, q), own_sem.at[q, axis, v])

    def multiply(q, first, last):
        def one(m, carry):
            axis, t = rem(m, 2), div(m, 2)
            i = t + div(t, 2) * (5 - 2 * t)
            spot = jnp.where(i == 0, 0, 3 * axis + i)

            @pl.when(m != 1)
            def _():
                arrival(q, spot, 1).wait_recv()

            left = jnp.concatenate(
                [
                    jnp.concatenate([blk[spot, other, c, q * half:(q + 1) * half] for c in range(CH)], axis=1)
                    for other in range(2)
                ],
                axis=0,
            )
            right = wfull[pl.ds(pl.multiple_of(axis * 2 * shard, 2 * shard), 2 * shard)]
            product = lax.dot_general(left, right, nt, preferred_element_type=jnp.float32).astype(jnp.bfloat16)
            for other in range(2):
                for v in range(2):
                    outs[q, axis, i, other, v] = product[other * half:(other + 1) * half, v * shard:(v + 1) * shard]
            for v in range(2):
                out_copy(q, axis, i, 1, v).start()

                @pl.when(i != 0)
                def _():
                    out_copy(q, axis, i, 0, v).start()

                @pl.when(i == 0)
                def _():
                    out_own(q, axis, v).start()
            return carry

        lax.fori_loop(first, last, one, 0)

    def share(q, spots):
        for k in spots:
            for axis in range(2):
                spot = 3 * axis + (2 if k == 2 else ways[q][1 - k])
                arrival(q, spot, 0).wait_recv()
                if k == 0:
                    onward(q, axis).start()
                across(q, spot).start()

    near = 2 * RG - 2
    share(0, (0, 1))
    share(1, (0, 1))
    multiply(0, 0, near)
    share(0, (2,))
    multiply(1, 0, near)
    multiply(0, near, 2 * RG)
    share(1, (2,))
    multiply(1, near, 2 * RG)

    mates(lambda kind, m: piece_out(kind, m).wait_send())
    mates(lambda kind, m: window_out(kind, m).wait_send())
    for i in range(1, RG):
        for kind in range(2):
            group_out(kind, i).wait_send()
    mates(lambda kind, m: term_out(kind, m).wait_send())
    mates(lambda kind, m: deliver(kind, m).wait_send())
    for kind in range(2):
        x_copy(kind).wait_send()
        for i in range(1, RG):
            total_out(kind, i).wait_send()
    w_shift.wait_send()
    for z in range(RG):
        @pl.when(w_target(z) != me)
        def _():
            w_out(z).wait_send()

    for q in range(HALVES):
        for axis in range(2):
            along(q, axis, 1).wait_send()
            along(q, axis, 3).wait_send()
            onward(q, axis).wait_send()
            for i in range(1, RG):
                across(q, 3 * axis + i).wait_send()
        across(q, 0).wait_send()
    for head in range(HK):
        wide_q = pl.ds(head * GROUP * HD, GROUP * HD)
        pltpu.make_async_copy(dq_s.at[:, wide_q], dq_hbm.at[:, wide_q], dq_sem.at[head]).wait()

    def finish(m, carry):
        axis, i = div(m, RG), rem(m, RG)
        for q in range(HALVES):
            for v in range(2):
                for other in range(2):
                    there = core + other * (1 - 2 * core)
                    incoming = remote(
                        outs.at[q, axis, i, other, v], out_part(chip(axis, i, there), axis, v, q),
                        os_.at[q, axis, i, other, v], or_.at[q, axis, i, other, v], ctx=sibling,
                    )

                    @pl.when(i + other > 0)
                    def _():
                        out_copy(q, axis, i, other, v).wait_send()
                        incoming.wait_recv()

                @pl.when(i == 0)
                def _():
                    out_own(q, axis, v).wait()
        return carry

    lax.fori_loop(0, 2 * RG, finish, 0)


def shards(queries, key_rows, value_rows, out_grad, kv_weight, doc_lengths, block_plan):
    n = lax.axis_size("ctx")
    sections = lax.axis_size("section")
    tokens, width = queries.shape[1:]
    features = kv_weight.shape[1]
    model = features * n
    share = model // CH
    hbm = pl.BlockSpec(memory_space=pltpu.HBM)
    anywhere = pl.BlockSpec(memory_space=pl.ANY)
    low = jnp.bfloat16
    dma = pltpu.SemaphoreType.DMA
    query_grad, input_grad = pl.pallas_call(
        functools.partial(kernel, n, sections),
        out_shape=(
            jax.ShapeDtypeStruct((tokens, width), low),
            jax.ShapeDtypeStruct((tokens, model), low),
        ),
        in_specs=[hbm] * 7,
        out_specs=(anywhere, anywhere),
        scratch_shapes=[
            pltpu.SMEM(doc_lengths.shape, jnp.int32),
            pltpu.SMEM((n,), jnp.int32),
            pltpu.SMEM((2, n), jnp.int32),
            pltpu.VMEM((tokens, width), low),
            pltpu.VMEM((tokens, width), low),
            pltpu.VMEM((tokens, width), low),
            pltpu.VMEM((CH, SLOTS, BLOCK, HD), low),
            pltpu.VMEM((2, n, BLOCK // 2, HD), low),
            pltpu.VMEM((2, CH, BACK, BLOCK // 2, HD), low),
            pltpu.VMEM((SLOTS * BLOCK, BLOCK), jnp.float32),
            pltpu.VMEM((SLOTS * BLOCK, GROUP * BLOCK), jnp.float32),
            pltpu.VMEM((SLOTS * BLOCK, GROUP * BLOCK), jnp.float32),
            pltpu.VMEM((CH, SLOTS, BLOCK, HD), low),
            pltpu.VMEM((2, CH + 1, SLOTS, BLOCK // 2, HD), low),
            pltpu.VMEM((2, n, BLOCK // 2, HD), low),
            pltpu.VMEM((2, RG, CH, BLOCK // 2, HD), low),
            pltpu.VMEM((2, CH, BLOCK // 2, HD), low),
            pltpu.VMEM((2, CH, BLOCK // 2, HD), low),
            pltpu.VMEM((7, 2, CH, BLOCK, HD), low),
            pltpu.VMEM((features, CH * HD), low),
            pltpu.VMEM((share, CH * HD), low),
            pltpu.VMEM((HALVES, 2, RG, 2, 2, BLOCK // HALVES, features), low),
            dma((4,)), dma((2, HK)), dma((HK,)),
            dma((2, CH)), dma((2, CH)), dma((2, RG)), dma((2, RG)), dma((2, CH)), dma((2, CH)), dma((2, CH)), dma((2, CH)),
            dma((2, RG)), dma((2, RG)), dma((2,)), dma((2,)), dma((2, CH)), dma((2, CH)),
            dma((HALVES, 14)), dma((HALVES, 7, 2)),
            dma((HALVES, 2, RG, 2, 2)), dma((HALVES, 2, RG, 2, 2)), dma((HALVES, 2, 2)),
            dma((7,)), dma, dma, dma((RG,)), dma((RG,)),
        ],
        compiler_params=pltpu.CompilerParams(
            collective_id=0, has_side_effects=True, vmem_limit_bytes=56 * 1024 * 1024
        ),
    )(doc_lengths, block_plan, queries[0], key_rows[0], value_rows[0], out_grad[0], kv_weight[0])
    return (query_grad[None], input_grad[None])


def solution(mesh):
    spec = P("section", "ctx", None)
    return jax.shard_map(
        shards, mesh=mesh, in_specs=(spec,) * 5 + (P(), P()), out_specs=(spec, spec), check_vma=False
    )
```

```python
import functools
import math

import jax
import jax.numpy as jnp
from jax import lax
from jax.experimental import pallas as pl
from jax.experimental.pallas import tpu as pltpu
from jax.sharding import PartitionSpec as P

HQ = 32
HK = 4
HD = 128
BLOCK = 128
GROUP = HQ // HK
BACK = 8
SLOTS = BACK + 1
CH = 2 * HK
SUB = 32
RG = BLOCK // SUB
MASKED = -1e30
MIX = 13
EARLY = 6
PARTS = 2
HALVES = 2
KEYS = 384
MESH = pl.DeviceIdType.MESH


def rem(a, b):
    return lax.rem(a, b)


def div(a, b):
    return lax.div(a, b)


def kernel(
    n, sections, lens_hbm, plan_hbm, q_hbm, k_hbm, v_hbm, o_hbm, w_hbm, dq_hbm, out_hbm,
    lens, plan, inv, q_s, o_s, dq_s, kvw, hold, send2, bias, s_s, g_s, part, terms, sums, totals, kvo, blk, wsh, wfull, outs,
    in_sem, kv_sem, dq_sem, s1s, s1r, g1s, g1r, s2s, s2r, s3s, s3r, rs, rr, ds_, dr, gs, gr, os_, or_, own_terms, own_sem, ready, loc_sem, wxs, wxr, wgs, wgr,
):
    me = lax.axis_index("ctx")
    sec = lax.axis_index("section")
    rg = div(me, CH)
    ch = rem(me, CH)
    core = rem(ch, 2)
    column = div(ch, 2)
    before = rem(sec + sections - 1, sections)

    def remote(src, dst, send, recv, **where):
        return pltpu.make_async_remote_copy(
            src_ref=src, dst_ref=dst, send_sem=send, recv_sem=recv,
            device_id=where, device_id_type=MESH,
        )

    load_lens = pltpu.make_async_copy(lens_hbm, lens, in_sem.at[2])
    load_plan = pltpu.make_async_copy(plan_hbm, plan, in_sem.at[3])
    load_q = pltpu.make_async_copy(q_hbm, q_s, in_sem.at[0])
    load_o = pltpu.make_async_copy(o_hbm, o_s, in_sem.at[1])
    load_kv = [
        pltpu.make_async_copy(
            (v_hbm if kind else k_hbm).at[:, pl.ds(head * HD, HD)], kvw.at[kind * HK + head, BACK], kv_sem.at[kind, head]
        )
        for kind in range(2)
        for head in range(HK)
    ]
    for load in (load_plan, load_lens, *load_kv, load_q, load_o):
        load.start()

    def device(z, y, core):
        return z * CH + 2 * y + core

    halves = BLOCK // 2
    line = (2 * column + core, 2 * rg + core)

    def mate(kind, m):
        return device(rg, div(m, 2), rem(m, 2)) if kind == 0 else device(div(m, 2), column, rem(m, 2))

    barrier = pltpu.get_barrier_semaphore()

    def greet(j):
        pl.semaphore_signal(barrier, inc=1, device_id={"ctx": j}, device_id_type=MESH)

    for k in range(1, CH):
        greet(mate(0, rem(line[0] + k, CH)))
    for k in range(1, RG):
        for there in range(2):
            greet(device(rem(rg + k, RG), column, there))
    after = rem(sec + 1, sections)
    for neighbour in (before, after):
        pl.semaphore_signal(barrier, inc=1, device_id={"section": neighbour}, device_id_type=MESH)
    load_plan.wait()
    load_lens.wait()

    def invert(b, carry):
        place = jnp.int32(0)
        for p in range(n):
            place = jnp.where(plan[p] == b, p, place)
        inv[0, b] = place
        inv[1, b] = rem(div(place, 2), RG) * CH + div(place, CH) * 2 + rem(place, 2)
        return carry

    lax.fori_loop(0, n, invert, 0)
    for load in load_kv:
        load.wait()
    pl.semaphore_wait(barrier, CH - 1 + 2 * (RG - 1) + 2)
    pl.semaphore_signal(ready, inc=1, device_id={"section": after}, device_id_type=MESH)

    def held_head(m):
        return rem(div(m, 2) + 2 * rem(m, 2), HK)

    def half_of(m):
        return pl.ds(pl.multiple_of(rem(m, 2) * halves, halves), halves)

    held = (me, column * CH + 2 * rg + core)

    def piece_out(kind, m):
        return remote(
            kvw.at[kind * HK + held_head(m), BACK, half_of(m)], hold.at[kind, held[kind]],
            s1s.at[kind, m], s1r.at[kind, line[kind]], ctx=mate(kind, m),
        )

    def piece_in(kind, m):
        return remote(
            kvw.at[0, BACK, half_of(0)], hold.at[kind, m if kind else rg * CH + m],
            s1s.at[kind, m], s1r.at[kind, m], ctx=mate(kind, m),
        )

    def mates(body):
        for k in range(1, CH):
            for kind in range(2):
                body(kind, rem(line[kind] + 3 * k, CH))

    for far in (0, 1, 3, 2):
        for there in ((1,) if far == 0 else (0, 1)):
            for kind in range(2):
                piece_out(kind, 2 * rem((rg if kind else column) + far, RG) + rem(core + there, 2)).start()
    w_shift = remote(w_hbm, wsh, wxs, wxr, section=before)
    w_shift.start()
    for kind in range(2):
        hold[kind, held[kind]] = kvw[kind * HK + held_head(line[kind]), BACK, half_of(line[kind])]

    token_block = plan[me]
    row_token = token_block * BLOCK + lax.broadcasted_iota(jnp.int32, (1, BLOCK), 1)
    start = jnp.zeros((1, BLOCK), jnp.int32)
    end = jnp.int32(0)
    for j in range(lens.shape[0]):
        end = end + lens[j]
        start = jnp.where(row_token >= end, end, start)
    key_token = (token_block - BACK) * BLOCK + lax.broadcasted_iota(jnp.int32, (SLOTS * BLOCK, BLOCK), 0)
    seen = jnp.logical_and(key_token >= start, key_token <= row_token)
    bias[...] = jnp.where(seen, 0.0, MASKED)
    for kind in range(2):
        terms[kind, CH] = jnp.zeros((SLOTS, halves, HD), jnp.bfloat16)

    def pair(kind, i, far):
        here, along_it = (rg, column) if kind == 0 else (column, rg)
        first = rem(here + i, RG) * CH + 2 * rem(along_it + far, RG)
        return hold.at[kind, pl.ds(pl.multiple_of(first, 2), 2)]

    def peer(kind, i):
        return device(rem(rg + i, RG), column, core) if kind == 0 else device(rg, rem(column + i, RG), core)

    def pair_out(kind, i, far):
        return remote(
            pair(kind, 0, far), pair(kind, 0, far), g1s.at[kind, i, far], g1r.at[kind, RG - i, far], ctx=peer(kind, i)
        )

    def pair_in(kind, i, far):
        return remote(
            pair(kind, i, far), pair(kind, i, far), g1s.at[kind, i, far], g1r.at[kind, i, far], ctx=peer(kind, i)
        )

    def came_from(kind, far, there):
        return 2 * rem((column if kind == 0 else rg) + far, RG) + there

    for far in (0, 1, 3, 2):
        for kind in range(2):
            if far:
                piece_in(kind, came_from(kind, far, core)).wait_recv()
            piece_in(kind, came_from(kind, far, 1 - core)).wait_recv()
            for i in (1, 3, 2):
                pair_out(kind, i, far).start()
    for far in (0, 1, 3, 2):
        for i in (1, 3, 2):
            for kind in range(2):
                pair_in(kind, i, far).wait_recv()

    def window_slots(kind, m):
        return kvw.at[kind * HK + held_head(m), pl.ds(0, BACK), half_of(m)]

    def window_out(kind, m):
        return remote(
            send2.at[kind, m], window_slots(kind, line[kind]), s2s.at[kind, m], s2r.at[kind, line[kind]], ctx=mate(kind, m)
        )

    def window_own(kind):
        return pltpu.make_async_copy(send2.at[kind, line[kind]], window_slots(kind, line[kind]), loc_sem.at[4 * kind])

    def window_in(kind, m):
        return remote(send2.at[kind, m], window_slots(kind, m), s2s.at[kind, m], s2r.at[kind, m], ctx=mate(kind, m))

    turn_of = rem(rg + column, HK)

    def window_step(i, carry):
        for kind in range(2):
            start_at = held_head(line[kind]) + 2 * RG - div(i, 2) - (rg if kind == 0 else column)
            m = 2 * rem(start_at, RG) + rem(i, 2)
            first = plan[mate(kind, m)] - BACK
            for w in range(BACK):
                send2[kind, m, w] = hold[kind, inv[kind, jnp.maximum(first + w, 0)]]

            @pl.when(m != line[kind])
            def _():
                window_out(kind, m).start()

            @pl.when(m == line[kind])
            def _():
                window_own(kind).start()
        return carry

    lax.fori_loop(0, CH, window_step, 0)

    place = rg * (1 - core) + column * core
    w_slot = 2 * core + rem(place, 2)
    shard = w_hbm.shape[0]

    def w_rows(slot):
        return wfull.at[pl.ds(pl.multiple_of(slot * shard, shard), shard)]

    def w_target(i):
        return device(i * (1 - core) + rg * core, column * (1 - core) + i * core, div(place, 2))

    def w_source(u):
        if u < 2:
            return device(2 * core + u, column, 0)
        return device(rg, 2 * core + u - 2, 1)

    def w_out(i):
        return remote(wsh, w_rows(w_slot), wgs.at[i], wgr.at[w_slot], ctx=w_target(i))

    def w_own():
        return pltpu.make_async_copy(wsh, w_rows(w_slot), loc_sem.at[1])

    def spread_weights():
        w_shift.wait_recv()
        for z in range(RG):
            @pl.when(w_target(z) != me)
            def _():
                w_out(z).start()

            @pl.when(w_target(z) == me)
            def _():
                w_own().start()

    load_q.wait()
    load_o.wait()

    scale = 1.0 / math.sqrt(HD)
    power = scale * math.log2(math.e)
    nt = (((1,), (1,)), ((), ()))
    tn = (((0,), (0,)), ((), ()))

    cuts = (pl.ds(0, EARLY), pl.ds(EARLY, SLOTS - EARLY))

    def term_out(kind, m, cut):
        return remote(
            part.at[kind * HK + held_head(m), cuts[cut], half_of(m)], terms.at[kind, line[kind], cuts[cut]],
            s3s.at[kind, m, cut], s3r.at[kind, line[kind], cut], ctx=mate(kind, m),
        )

    def term_own(kind, cut):
        m = line[kind]
        return pltpu.make_async_copy(
            part.at[kind * HK + held_head(m), cuts[cut], half_of(m)], terms.at[kind, m, cuts[cut]], own_terms.at[kind, cut]
        )

    def term_in(kind, m, cut):
        return remote(
            part.at[0, cuts[cut], half_of(0)], terms.at[kind, m, cuts[cut]],
            s3s.at[kind, m, cut], s3r.at[kind, m, cut], ctx=mate(kind, m),
        )

    def send_terms(head, cut):
        for half in range(2):
            m = 2 * rem(head + RG - 2 * half, RG) + half
            for kind in range(2):
                @pl.when(m != line[kind])
                def _():
                    term_out(kind, m, cut).start()

                @pl.when(m == line[kind])
                def _():
                    term_own(kind, cut).start()

    def one_head(step, carry):
        head = rem(step + turn_of, HK)
        for half in range(2):
            m = 2 * rem(head + RG - 2 * half, RG) + half
            for kind in range(2):
                @pl.when(m != line[kind])
                def _():
                    window_in(kind, m).wait_recv()

                @pl.when(m == line[kind])
                def _():
                    window_own(kind).wait()

        @pl.when(step == 1)
        def _():
            spread_weights()

        def columns(i):
            return pl.ds(pl.multiple_of((head * GROUP + i) * HD, HD), HD)

        q2 = jnp.concatenate([q_s[:, columns(i)] for i in range(GROUP)], axis=0)
        o2 = jnp.concatenate([o_s[:, columns(i)] for i in range(GROUP)], axis=0)
        wide = GROUP * BLOCK
        spans = [(slice(i, i + KEYS), slice(i // BLOCK, (i + KEYS) // BLOCK)) for i in range(0, SLOTS * BLOCK, KEYS)]

        def folded(x, over):
            return over(x.reshape(KEYS // 8, 8, wide), axis=0)

        peak = None
        for span, slots in spans:
            b = bias[span]
            keys = kvw[head, slots].reshape(KEYS, HD)
            scores = lax.dot_general(keys, q2, nt, preferred_element_type=jnp.float32)
            scores = scores + jnp.concatenate([b] * GROUP, axis=1)
            s_s[span] = scores
            top = folded(scores, jnp.max)
            peak = top if peak is None else jnp.maximum(peak, top)
            values = kvw[HK + head, slots].reshape(KEYS, HD)
            g_s[span] = lax.dot_general(values, o2, nt, preferred_element_type=jnp.float32)
        peak = jnp.max(peak, axis=0, keepdims=True)
        total = jnp.zeros((8, wide), jnp.float32)
        weighted = jnp.zeros((8, wide), jnp.float32)
        for span, slots in spans:
            terms = jnp.exp2((s_s[span] - peak) * power)
            s_s[span] = terms
            total = total + folded(terms, jnp.sum)
            weighted = weighted + folded(terms * g_s[span], jnp.sum)
        inverse = 1.0 / jnp.sum(total, axis=0, keepdims=True)
        delta = jnp.sum(weighted, axis=0, keepdims=True) * inverse
        dq = jnp.zeros((wide, HD), jnp.float32)
        for span, slots in spans:
            prob = s_s[span] * inverse
            prob_low = prob.astype(jnp.bfloat16)
            score_low = (prob * (g_s[span] - delta)).astype(jnp.bfloat16)
            dv = jnp.dot(prob_low, o2, preferred_element_type=jnp.float32)
            dk = jnp.dot(score_low, q2, preferred_element_type=jnp.float32) * scale
            part[HK + head, slots] = dv.astype(jnp.bfloat16).reshape(KEYS // BLOCK, BLOCK, HD)
            part[head, slots] = dk.astype(jnp.bfloat16).reshape(KEYS // BLOCK, BLOCK, HD)
            keys = kvw[head, slots].reshape(KEYS, HD)
            dq = dq + lax.dot_general(score_low, keys, tn, preferred_element_type=jnp.float32)
            if slots.stop == EARLY:
                send_terms(head, 0)
        for i in range(GROUP):
            dq_s[:, columns(i)] = (dq[i * BLOCK:(i + 1) * BLOCK] * scale).astype(jnp.bfloat16)

        send_terms(head, 1)
        wide = pl.ds(pl.multiple_of(head * GROUP * HD, GROUP * HD), GROUP * HD)
        pltpu.make_async_copy(dq_s.at[:, wide], dq_hbm.at[:, wide], dq_sem.at[head]).start()
        return carry

    lax.fori_loop(0, HK, one_head, 0)

    for cut in range(2):
        mates(lambda kind, m: term_in(kind, m, cut).wait_recv())
        for kind in range(2):
            term_own(kind, cut).wait()

    step_of = CH // PARTS

    def some(first, part_no):
        return pl.ds(pl.multiple_of(first * CH + part_no * step_of, step_of), step_of)

    def total_out(kind, i, c):
        to = rem((rg if kind == 0 else column) + i, RG)
        return remote(
            sums.at[kind, some(to, c)], totals.at[kind, RG - i, some(0, c)],
            rs.at[kind, i, c], rr.at[kind, RG - i, c], ctx=peer(kind, i),
        )

    def total_in(kind, i, c):
        return remote(
            sums.at[kind, some(0, c)], totals.at[kind, i, some(0, c)], rs.at[kind, i, c], rr.at[kind, i, c], ctx=peer(kind, i)
        )

    for c in range(PARTS):
        for i in (1, 3, 2, 0):
            for kind in range(2):
                here = rg if kind == 0 else column
                to = rem(here + i, RG)

                def one_block(e, carry):
                    p = device(to, div(e, 2), rem(e, 2)) if kind == 0 else device(div(e, 2), to, rem(e, 2))
                    total = jnp.zeros((halves, HD), jnp.float32)
                    for w in range(SLOTS):
                        later = plan[p] + BACK - w
                        source = inv[kind, jnp.minimum(later, n - 1)]
                        wanted = jnp.logical_and(later < n, div(source, CH) == here)
                        total = total + terms[kind, jnp.where(wanted, rem(source, CH), CH), w].astype(jnp.float32)
                    sums[kind, to * CH + e] = total.astype(jnp.bfloat16)
                    return carry

                lax.fori_loop(c * step_of, (c + 1) * step_of, one_block, 0)
                if i > 0:
                    total_out(kind, i, c).start()

    def owned(kind, m):
        return blk.at[0, 0, kind * HK + held_head(m), half_of(m)]

    def deliver(kind, m):
        return remote(
            kvo.at[kind, m], owned(kind, line[kind]), ds_.at[kind, m], dr.at[kind, line[kind]],
            section=before, ctx=mate(kind, m),
        )

    def delivered(kind, m):
        return remote(kvo.at[kind, m], owned(kind, m), ds_.at[kind, m], dr.at[kind, m], section=before, ctx=mate(kind, m))

    pl.semaphore_wait(ready, 1)
    for c in range(PARTS):
        for kind in range(2):
            here = rg if kind == 0 else column
            for i in range(1, RG):
                total_in(kind, i, c).wait_recv()

            def one_sum(e, carry):
                total = sums[kind, here * CH + c * step_of + e].astype(jnp.float32)
                for i in range(1, RG):
                    total = total + totals[kind, i, c * step_of + e].astype(jnp.float32)
                kvo[kind, c * step_of + e] = total.astype(jnp.bfloat16)
                return carry

            lax.fori_loop(0, step_of, one_sum, 0)
        for e in range(step_of):
            for kind in range(2):
                deliver(kind, c * step_of + rem(e + line[kind], step_of)).start()

    for m in range(CH):
        for kind in range(2):
            delivered(kind, m).wait_recv()

    sibling = device(rg, column, 1 - core)
    half = BLOCK // HALVES

    def half_rows(q):
        return pl.ds(pl.multiple_of(q * half, half), half)

    def chip(axis, i, core):
        return device(rem(rg + axis * i, RG), rem(column + (1 - axis) * i, RG), core)

    def along(q, axis, i):
        return remote(
            blk.at[0, 0, :, half_rows(q)], blk.at[3 * axis + RG - i, 0, :, half_rows(q)],
            gs.at[q, 3 * axis + i], gr.at[q, 3 * axis + RG - i, 0], ctx=chip(axis, i, core),
        )

    def across(q, spot):
        return remote(
            blk.at[spot, 0, :, half_rows(q)], blk.at[spot, 1, :, half_rows(q)],
            gs.at[q, 7 + spot], gr.at[q, spot, 1], ctx=sibling,
        )

    def arrival(q, spot, other):
        return remote(
            blk.at[spot, other, :, half_rows(q)], blk.at[spot, other, :, half_rows(q)],
            gs.at[q, 0], gr.at[q, spot, other], ctx=sibling,
        )

    ways = ((1, 3), (3, 1))

    def onward(q, axis):
        to, source = ways[q]
        return remote(
            blk.at[3 * axis + source, 0, :, half_rows(q)], blk.at[3 * axis + 2, 0, :, half_rows(q)],
            gs.at[q, 3 * axis + 2], gr.at[q, 3 * axis + 2, 0], ctx=chip(axis, to, core),
        )

    for q in range(HALVES):
        for k in range(2):
            for axis in range(2):
                along(q, axis, ways[q][k]).start()
        across(q, 0).start()

    for u in range(RG):
        @pl.when(w_source(u) != me)
        def _():
            remote(wsh, w_rows(u), wgs.at[u], wgr.at[u], ctx=w_source(u)).wait_recv()

        @pl.when(w_source(u) == me)
        def _():
            w_own().wait()

    def out_part(j, axis, v, q):
        z, y, b = div(j, CH), rem(div(j, 2), RG), rem(j, 2)
        number = (1 - axis) * device(2 * b + v, y, 0) + axis * device(z, 2 * b + v, 1)
        return out_hbm.at[half_rows(q), pl.ds(pl.multiple_of(number * shard, shard), shard)]

    def out_copy(q, axis, i, other, v):
        core_there = core + other * (1 - 2 * core)
        return remote(
            outs.at[q, axis, i, other, v], out_part(me, axis, v, q),
            os_.at[q, axis, i, other, v], or_.at[q, axis, rem(RG - i, RG), other, v], ctx=chip(axis, i, core_there),
        )

    def out_own(q, axis, v):
        return pltpu.make_async_copy(outs.at[q, axis, 0, 0, v], out_part(me, axis, v, q), own_sem.at[q, axis, v])

    def multiply(q, first, last):
        def one(m, carry):
            axis, t = rem(m, 2), div(m, 2)
            i = t + div(t, 2) * (5 - 2 * t)
            spot = jnp.where(i == 0, 0, 3 * axis + i)

            @pl.when(m != 1)
            def _():
                arrival(q, spot, 1).wait_recv()

            left = jnp.concatenate(
                [
                    jnp.concatenate([blk[spot, other, c, q * half:(q + 1) * half] for c in range(CH)], axis=1)
                    for other in range(2)
                ],
                axis=0,
            )
            right = wfull[pl.ds(pl.multiple_of(axis * 2 * shard, 2 * shard), 2 * shard)]
            product = lax.dot_general(left, right, nt, preferred_element_type=jnp.float32).astype(jnp.bfloat16)
            for other in range(2):
                for v in range(2):
                    outs[q, axis, i, other, v] = product[other * half:(other + 1) * half, v * shard:(v + 1) * shard]
            for v in range(2):
                out_copy(q, axis, i, 1, v).start()

                @pl.when(i != 0)
                def _():
                    out_copy(q, axis, i, 0, v).start()

                @pl.when(i == 0)
                def _():
                    out_own(q, axis, v).start()
            return carry

        lax.fori_loop(first, last, one, 0)

    def share(q, spots):
        for k in spots:
            for axis in range(2):
                spot = 3 * axis + (2 if k == 2 else ways[q][1 - k])
                arrival(q, spot, 0).wait_recv()
                if k == 0:
                    onward(q, axis).start()
                across(q, spot).start()

    near = 2 * RG - 2
    share(0, (0, 1))
    share(1, (0, 1))
    multiply(0, 0, near)
    share(0, (2,))
    multiply(1, 0, near)
    multiply(0, near, 2 * RG)
    share(1, (2,))
    multiply(1, near, 2 * RG)

    mates(lambda kind, m: piece_out(kind, m).wait_send())
    mates(lambda kind, m: window_out(kind, m).wait_send())
    for far in range(RG):
        for i in range(1, RG):
            for kind in range(2):
                pair_out(kind, i, far).wait_send()
    for cut in range(2):
        mates(lambda kind, m: term_out(kind, m, cut).wait_send())
    for kind in range(2):
        for m in range(CH):
            deliver(kind, m).wait_send()
        for c in range(PARTS):
            for i in range(1, RG):
                total_out(kind, i, c).wait_send()
    w_shift.wait_send()
    for z in range(RG):
        @pl.when(w_target(z) != me)
        def _():
            w_out(z).wait_send()

    for q in range(HALVES):
        for axis in range(2):
            along(q, axis, 1).wait_send()
            along(q, axis, 3).wait_send()
            onward(q, axis).wait_send()
            for i in range(1, RG):
                across(q, 3 * axis + i).wait_send()
        across(q, 0).wait_send()
    for head in range(HK):
        wide_q = pl.ds(head * GROUP * HD, GROUP * HD)
        pltpu.make_async_copy(dq_s.at[:, wide_q], dq_hbm.at[:, wide_q], dq_sem.at[head]).wait()

    def finish(m, carry):
        axis, i = div(m, RG), rem(m, RG)
        for q in range(HALVES):
            for v in range(2):
                for other in range(2):
                    there = core + other * (1 - 2 * core)
                    incoming = remote(
                        outs.at[q, axis, i, other, v], out_part(chip(axis, i, there), axis, v, q),
                        os_.at[q, axis, i, other, v], or_.at[q, axis, i, other, v], ctx=sibling,
                    )

                    @pl.when(i + other > 0)
                    def _():
                        out_copy(q, axis, i, other, v).wait_send()
                        incoming.wait_recv()

                @pl.when(i == 0)
                def _():
                    out_own(q, axis, v).wait()
        return carry

    lax.fori_loop(0, 2 * RG, finish, 0)


def shards(queries, key_rows, value_rows, out_grad, kv_weight, doc_lengths, block_plan):
    n = lax.axis_size("ctx")
    sections = lax.axis_size("section")
    tokens, width = queries.shape[1:]
    features = kv_weight.shape[1]
    model = features * n
    share = model // CH
    hbm = pl.BlockSpec(memory_space=pltpu.HBM)
    anywhere = pl.BlockSpec(memory_space=pl.ANY)
    low = jnp.bfloat16
    dma = pltpu.SemaphoreType.DMA
    query_grad, input_grad = pl.pallas_call(
        functools.partial(kernel, n, sections),
        out_shape=(
            jax.ShapeDtypeStruct((tokens, width), low),
            jax.ShapeDtypeStruct((tokens, model), low),
        ),
        in_specs=[hbm] * 7,
        out_specs=(anywhere, anywhere),
        scratch_shapes=[
            pltpu.SMEM(doc_lengths.shape, jnp.int32),
            pltpu.SMEM((n,), jnp.int32),
            pltpu.SMEM((2, n), jnp.int32),
            pltpu.VMEM((tokens, width), low),
            pltpu.VMEM((tokens, width), low),
            pltpu.VMEM((tokens, width), low),
            pltpu.VMEM((CH, SLOTS, BLOCK, HD), low),
            pltpu.VMEM((2, n, BLOCK // 2, HD), low),
            pltpu.VMEM((2, CH, BACK, BLOCK // 2, HD), low),
            pltpu.VMEM((SLOTS * BLOCK, BLOCK), jnp.float32),
            pltpu.VMEM((SLOTS * BLOCK, GROUP * BLOCK), jnp.float32),
            pltpu.VMEM((SLOTS * BLOCK, GROUP * BLOCK), jnp.float32),
            pltpu.VMEM((CH, SLOTS, BLOCK, HD), low),
            pltpu.VMEM((2, CH + 1, SLOTS, BLOCK // 2, HD), low),
            pltpu.VMEM((2, n, BLOCK // 2, HD), low),
            pltpu.VMEM((2, RG, CH, BLOCK // 2, HD), low),
            pltpu.VMEM((2, CH, BLOCK // 2, HD), low),
            pltpu.VMEM((7, 2, CH, BLOCK, HD), low),
            pltpu.VMEM((features, CH * HD), low),
            pltpu.VMEM((share, CH * HD), low),
            pltpu.VMEM((HALVES, 2, RG, 2, 2, BLOCK // HALVES, features), low),
            dma((4,)), dma((2, HK)), dma((HK,)),
            dma((2, CH)), dma((2, CH)), dma((2, RG, RG)), dma((2, RG, RG)), dma((2, CH)), dma((2, CH)),
            dma((2, CH, 2)), dma((2, CH, 2)),
            dma((2, RG, PARTS)), dma((2, RG, PARTS)), dma((2, CH)), dma((2, CH)),
            dma((HALVES, 14)), dma((HALVES, 7, 2)),
            dma((HALVES, 2, RG, 2, 2)), dma((HALVES, 2, RG, 2, 2)), dma((2, 2)), dma((HALVES, 2, 2)),
            pltpu.SemaphoreType.REGULAR, dma((7,)), dma, dma, dma((RG,)), dma((RG,)),
        ],
        compiler_params=pltpu.CompilerParams(
            collective_id=0, has_side_effects=True, vmem_limit_bytes=56 * 1024 * 1024
        ),
    )(doc_lengths, block_plan, queries[0], key_rows[0], value_rows[0], out_grad[0], kv_weight[0])
    return (query_grad[None], input_grad[None])


def solution(mesh):
    spec = P("section", "ctx", None)
    return jax.shard_map(
        shards, mesh=mesh, in_specs=(spec,) * 5 + (P(), P()), out_specs=(spec, spec), check_vma=False
    )
```

```python
import functools
import math

import jax
import jax.numpy as jnp
from jax import lax
from jax.experimental import pallas as pl
from jax.experimental.pallas import tpu as pltpu
from jax.sharding import PartitionSpec as P

HQ = 32
HK = 4
HD = 128
BLOCK = 128
GROUP = HQ // HK
BACK = 8
SLOTS = BACK + 1
CH = 2 * HK
SUB = 32
RG = BLOCK // SUB
MASKED = -1e30
MIX = 13
EARLY = 6
PARTS = 2
HALVES = 2
KEYS = 384
MESH = pl.DeviceIdType.MESH


def rem(a, b):
    return lax.rem(a, b)


def div(a, b):
    return lax.div(a, b)


def kernel(
    n, sections, lens_hbm, plan_hbm, q_hbm, k_hbm, v_hbm, o_hbm, w_hbm, dq_hbm, out_hbm,
    lens, plan, inv, q_s, o_s, dq_s, kvw, hold, send2, bias, s_s, g_s, part, terms, sums, totals, kvo, blk, wsh, wfull, outs,
    in_sem, kv_sem, dq_sem, s1s, s1r, g1s, g1r, s2s, s2r, s3s, s3r, rs, rr, ds_, dr, gs, gr, os_, or_, own_terms, own_sem, ready, loc_sem, wxs, wxr, wgs, wgr,
):
    me = lax.axis_index("ctx")
    sec = lax.axis_index("section")
    rg = div(me, CH)
    ch = rem(me, CH)
    core = rem(ch, 2)
    column = div(ch, 2)
    before = rem(sec + sections - 1, sections)

    def remote(src, dst, send, recv, **where):
        return pltpu.make_async_remote_copy(
            src_ref=src, dst_ref=dst, send_sem=send, recv_sem=recv,
            device_id=where, device_id_type=MESH,
        )

    load_lens = pltpu.make_async_copy(lens_hbm, lens, in_sem.at[2])
    load_plan = pltpu.make_async_copy(plan_hbm, plan, in_sem.at[3])
    load_q = pltpu.make_async_copy(q_hbm, q_s, in_sem.at[0])
    load_o = pltpu.make_async_copy(o_hbm, o_s, in_sem.at[1])
    load_kv = [
        pltpu.make_async_copy(
            (v_hbm if kind else k_hbm).at[:, pl.ds(head * HD, HD)], kvw.at[kind * HK + head, BACK], kv_sem.at[kind, head]
        )
        for kind in range(2)
        for head in range(HK)
    ]
    for load in (load_plan, load_lens, *load_kv, load_q, load_o):
        load.start()

    def device(z, y, core):
        return z * CH + 2 * y + core

    halves = BLOCK // 2
    line = (2 * column + core, 2 * rg + core)

    def mate(kind, m):
        return device(rg, div(m, 2), rem(m, 2)) if kind == 0 else device(div(m, 2), column, rem(m, 2))

    barrier = pltpu.get_barrier_semaphore()

    def greet(j):
        pl.semaphore_signal(barrier, inc=1, device_id={"ctx": j}, device_id_type=MESH)

    for k in range(1, CH):
        greet(mate(0, rem(line[0] + k, CH)))
    for k in range(1, RG):
        for there in range(2):
            greet(device(rem(rg + k, RG), column, there))
    after = rem(sec + 1, sections)
    for neighbour in (before, after):
        pl.semaphore_signal(barrier, inc=1, device_id={"section": neighbour}, device_id_type=MESH)
    load_plan.wait()
    load_lens.wait()

    def invert(b, carry):
        place = jnp.int32(0)
        for p in range(n):
            place = jnp.where(plan[p] == b, p, place)
        inv[0, b] = place
        inv[1, b] = rem(div(place, 2), RG) * CH + div(place, CH) * 2 + rem(place, 2)
        return carry

    lax.fori_loop(0, n, invert, 0)
    for load in load_kv:
        load.wait()
    pl.semaphore_wait(barrier, CH - 1 + 2 * (RG - 1) + 2)
    pl.semaphore_signal(ready, inc=1, device_id={"section": after}, device_id_type=MESH)

    def held_head(m):
        return rem(div(m, 2) + 2 * rem(m, 2), HK)

    def half_of(m):
        return pl.ds(pl.multiple_of(rem(m, 2) * halves, halves), halves)

    held = (me, column * CH + 2 * rg + core)

    def piece_out(kind, m):
        return remote(
            kvw.at[kind * HK + held_head(m), BACK, half_of(m)], hold.at[kind, held[kind]],
            s1s.at[kind, m], s1r.at[kind, line[kind]], ctx=mate(kind, m),
        )

    def piece_in(kind, m):
        return remote(
            kvw.at[0, BACK, half_of(0)], hold.at[kind, m if kind else rg * CH + m],
            s1s.at[kind, m], s1r.at[kind, m], ctx=mate(kind, m),
        )

    def mates(body):
        for k in range(1, CH):
            for kind in range(2):
                body(kind, rem(line[kind] + 3 * k, CH))

    for far in (0, 1, 3, 2):
        for there in ((1,) if far == 0 else (0, 1)):
            for kind in range(2):
                piece_out(kind, 2 * rem((rg if kind else column) + far, RG) + rem(core + there, 2)).start()
    w_shift = remote(w_hbm, wsh, wxs, wxr, section=before)
    w_shift.start()
    for kind in range(2):
        hold[kind, held[kind]] = kvw[kind * HK + held_head(line[kind]), BACK, half_of(line[kind])]

    token_block = plan[me]
    row_token = token_block * BLOCK + lax.broadcasted_iota(jnp.int32, (1, BLOCK), 1)
    start = jnp.zeros((1, BLOCK), jnp.int32)
    end = jnp.int32(0)
    for j in range(lens.shape[0]):
        end = end + lens[j]
        start = jnp.where(row_token >= end, end, start)
    key_token = (token_block - BACK) * BLOCK + lax.broadcasted_iota(jnp.int32, (SLOTS * BLOCK, BLOCK), 0)
    seen = jnp.logical_and(key_token >= start, key_token <= row_token)
    bias[...] = jnp.where(seen, 0.0, MASKED)
    for kind in range(2):
        terms[kind, CH] = jnp.zeros((SLOTS, halves, HD), jnp.bfloat16)

    def pair(kind, i, far):
        here, along_it = (rg, column) if kind == 0 else (column, rg)
        first = rem(here + i, RG) * CH + 2 * rem(along_it + far, RG)
        return hold.at[kind, pl.ds(pl.multiple_of(first, 2), 2)]

    def peer(kind, i):
        return device(rem(rg + i, RG), column, core) if kind == 0 else device(rg, rem(column + i, RG), core)

    def pair_out(kind, i, far):
        return remote(
            pair(kind, 0, far), pair(kind, 0, far), g1s.at[kind, i, far], g1r.at[kind, RG - i, far], ctx=peer(kind, i)
        )

    def pair_in(kind, i, far):
        return remote(
            pair(kind, i, far), pair(kind, i, far), g1s.at[kind, i, far], g1r.at[kind, i, far], ctx=peer(kind, i)
        )

    def came_from(kind, far, there):
        return 2 * rem((column if kind == 0 else rg) + far, RG) + there

    for far in (0, 1, 3, 2):
        for kind in range(2):
            if far:
                piece_in(kind, came_from(kind, far, core)).wait_recv()
            piece_in(kind, came_from(kind, far, 1 - core)).wait_recv()
            for i in (1, 3, 2):
                pair_out(kind, i, far).start()
    for far in (0, 1, 3, 2):
        for i in (1, 3, 2):
            for kind in range(2):
                pair_in(kind, i, far).wait_recv()

    def window_slots(kind, m):
        return kvw.at[kind * HK + held_head(m), pl.ds(0, BACK), half_of(m)]

    def window_out(kind, m):
        return remote(
            send2.at[kind, m], window_slots(kind, line[kind]), s2s.at[kind, m], s2r.at[kind, line[kind]], ctx=mate(kind, m)
        )

    def window_own(kind):
        return pltpu.make_async_copy(send2.at[kind, line[kind]], window_slots(kind, line[kind]), loc_sem.at[4 * kind])

    def window_in(kind, m):
        return remote(send2.at[kind, m], window_slots(kind, m), s2s.at[kind, m], s2r.at[kind, m], ctx=mate(kind, m))

    turn_of = rem(rg + column, HK)

    def window_step(i, carry):
        for kind in range(2):
            start_at = held_head(line[kind]) + 2 * RG - div(i, 2) - (rg if kind == 0 else column)
            m = 2 * rem(start_at, RG) + rem(i, 2)
            first = plan[mate(kind, m)] - BACK
            for w in range(BACK):
                send2[kind, m, w] = hold[kind, inv[kind, jnp.maximum(first + w, 0)]]

            @pl.when(m != line[kind])
            def _():
                window_out(kind, m).start()

            @pl.when(m == line[kind])
            def _():
                window_own(kind).start()
        return carry

    lax.fori_loop(0, CH, window_step, 0)

    place = rg * (1 - core) + column * core
    w_slot = 2 * core + rem(place, 2)
    shard = w_hbm.shape[0]

    def w_rows(slot):
        return wfull.at[pl.ds(pl.multiple_of(slot * shard, shard), shard)]

    def w_target(i):
        return device(i * (1 - core) + rg * core, column * (1 - core) + i * core, div(place, 2))

    def w_source(u):
        if u < 2:
            return device(2 * core + u, column, 0)
        return device(rg, 2 * core + u - 2, 1)

    def w_out(i):
        return remote(wsh, w_rows(w_slot), wgs.at[i], wgr.at[w_slot], ctx=w_target(i))

    def w_own():
        return pltpu.make_async_copy(wsh, w_rows(w_slot), loc_sem.at[1])

    def spread_weights():
        w_shift.wait_recv()
        for z in range(RG):
            @pl.when(w_target(z) != me)
            def _():
                w_out(z).start()

            @pl.when(w_target(z) == me)
            def _():
                w_own().start()

    load_q.wait()
    load_o.wait()

    scale = 1.0 / math.sqrt(HD)
    power = scale * math.log2(math.e)
    nt = (((1,), (1,)), ((), ()))
    tn = (((0,), (0,)), ((), ()))

    cuts = (pl.ds(0, EARLY), pl.ds(EARLY, SLOTS - EARLY))

    def term_out(kind, m, cut):
        return remote(
            part.at[kind * HK + held_head(m), cuts[cut], half_of(m)], terms.at[kind, line[kind], cuts[cut]],
            s3s.at[kind, m, cut], s3r.at[kind, line[kind], cut], ctx=mate(kind, m),
        )

    def term_own(kind, cut):
        m = line[kind]
        return pltpu.make_async_copy(
            part.at[kind * HK + held_head(m), cuts[cut], half_of(m)], terms.at[kind, m, cuts[cut]], own_terms.at[kind, cut]
        )

    def term_in(kind, m, cut):
        return remote(
            part.at[0, cuts[cut], half_of(0)], terms.at[kind, m, cuts[cut]],
            s3s.at[kind, m, cut], s3r.at[kind, m, cut], ctx=mate(kind, m),
        )

    def send_terms(head, cut):
        for half in range(2):
            m = 2 * rem(head + RG - 2 * half, RG) + half
            for kind in range(2):
                @pl.when(m != line[kind])
                def _():
                    term_out(kind, m, cut).start()

                @pl.when(m == line[kind])
                def _():
                    term_own(kind, cut).start()

    def one_head(step, carry):
        head = rem(step + turn_of, HK)
        for half in range(2):
            m = 2 * rem(head + RG - 2 * half, RG) + half
            for kind in range(2):
                @pl.when(m != line[kind])
                def _():
                    window_in(kind, m).wait_recv()

                @pl.when(m == line[kind])
                def _():
                    window_own(kind).wait()

        @pl.when(step == 0)
        def _():
            spread_weights()

        def columns(i):
            return pl.ds(pl.multiple_of((head * GROUP + i) * HD, HD), HD)

        q2 = jnp.concatenate([q_s[:, columns(i)] for i in range(GROUP)], axis=0)
        o2 = jnp.concatenate([o_s[:, columns(i)] for i in range(GROUP)], axis=0)
        wide = GROUP * BLOCK
        spans = [(slice(i, i + KEYS), slice(i // BLOCK, (i + KEYS) // BLOCK)) for i in range(0, SLOTS * BLOCK, KEYS)]

        def folded(x, over):
            return over(x.reshape(KEYS // 8, 8, wide), axis=0)

        peak = None
        for span, slots in spans:
            b = bias[span]
            keys = kvw[head, slots].reshape(KEYS, HD)
            scores = lax.dot_general(keys, q2, nt, preferred_element_type=jnp.float32)
            scores = scores + jnp.concatenate([b] * GROUP, axis=1)
            s_s[span] = scores
            top = folded(scores, jnp.max)
            peak = top if peak is None else jnp.maximum(peak, top)
        peak = jnp.max(peak, axis=0, keepdims=True)
        total = jnp.zeros((8, wide), jnp.float32)
        weighted = jnp.zeros((8, wide), jnp.float32)
        for span, slots in spans:
            terms = jnp.exp2((s_s[span] - peak) * power)
            s_s[span] = terms
            total = total + folded(terms, jnp.sum)
            values = kvw[HK + head, slots].reshape(KEYS, HD)
            grads = lax.dot_general(values, o2, nt, preferred_element_type=jnp.float32)
            g_s[span] = grads
            weighted = weighted + folded(terms * grads, jnp.sum)
        inverse = 1.0 / jnp.sum(total, axis=0, keepdims=True)
        delta = jnp.sum(weighted, axis=0, keepdims=True) * inverse
        dq = jnp.zeros((wide, HD), jnp.float32)
        for span, slots in spans:
            prob = s_s[span] * inverse
            prob_low = prob.astype(jnp.bfloat16)
            score_low = (prob * (g_s[span] - delta)).astype(jnp.bfloat16)
            dv = jnp.dot(prob_low, o2, preferred_element_type=jnp.float32)
            dk = jnp.dot(score_low, q2, preferred_element_type=jnp.float32) * scale
            part[HK + head, slots] = dv.astype(jnp.bfloat16).reshape(KEYS // BLOCK, BLOCK, HD)
            part[head, slots] = dk.astype(jnp.bfloat16).reshape(KEYS // BLOCK, BLOCK, HD)
            keys = kvw[head, slots].reshape(KEYS, HD)
            dq = dq + lax.dot_general(score_low, keys, tn, preferred_element_type=jnp.float32)
            if slots.stop == EARLY:
                send_terms(head, 0)
        for i in range(GROUP):
            dq_s[:, columns(i)] = (dq[i * BLOCK:(i + 1) * BLOCK] * scale).astype(jnp.bfloat16)

        send_terms(head, 1)
        wide = pl.ds(pl.multiple_of(head * GROUP * HD, GROUP * HD), GROUP * HD)
        pltpu.make_async_copy(dq_s.at[:, wide], dq_hbm.at[:, wide], dq_sem.at[head]).start()
        return carry

    lax.fori_loop(0, HK, one_head, 0)

    for cut in range(2):
        mates(lambda kind, m: term_in(kind, m, cut).wait_recv())
        for kind in range(2):
            term_own(kind, cut).wait()

    step_of = CH // PARTS

    def some(first, part_no):
        return pl.ds(pl.multiple_of(first * CH + part_no * step_of, step_of), step_of)

    def total_out(kind, i, c):
        to = rem((rg if kind == 0 else column) + i, RG)
        return remote(
            sums.at[kind, some(to, c)], totals.at[kind, RG - i, some(0, c)],
            rs.at[kind, i, c], rr.at[kind, RG - i, c], ctx=peer(kind, i),
        )

    def total_in(kind, i, c):
        return remote(
            sums.at[kind, some(0, c)], totals.at[kind, i, some(0, c)], rs.at[kind, i, c], rr.at[kind, i, c], ctx=peer(kind, i)
        )

    for c in range(PARTS):
        for i in (2, 1, 3, 0):
            for kind in range(2):
                here = rg if kind == 0 else column
                to = rem(here + i, RG)

                def one_block(e, carry):
                    p = device(to, div(e, 2), rem(e, 2)) if kind == 0 else device(div(e, 2), to, rem(e, 2))
                    total = jnp.zeros((halves, HD), jnp.float32)
                    for w in range(SLOTS):
                        later = plan[p] + BACK - w
                        source = inv[kind, jnp.minimum(later, n - 1)]
                        wanted = jnp.logical_and(later < n, div(source, CH) == here)
                        total = total + terms[kind, jnp.where(wanted, rem(source, CH), CH), w].astype(jnp.float32)
                    sums[kind, to * CH + e] = total.astype(jnp.bfloat16)
                    return carry

                lax.fori_loop(c * step_of, (c + 1) * step_of, one_block, 0)
                if i > 0:
                    total_out(kind, i, c).start()

    def owned(kind, m):
        return blk.at[0, 0, kind * HK + held_head(m), half_of(m)]

    def deliver(kind, m):
        return remote(
            kvo.at[kind, m], owned(kind, line[kind]), ds_.at[kind, m], dr.at[kind, line[kind]],
            section=before, ctx=mate(kind, m),
        )

    def delivered(kind, m):
        return remote(kvo.at[kind, m], owned(kind, m), ds_.at[kind, m], dr.at[kind, m], section=before, ctx=mate(kind, m))

    pl.semaphore_wait(ready, 1)
    for c in range(PARTS):
        for kind in range(2):
            here = rg if kind == 0 else column
            for i in range(1, RG):
                total_in(kind, i, c).wait_recv()

            def one_sum(e, carry):
                total = sums[kind, here * CH + c * step_of + e].astype(jnp.float32)
                for i in range(1, RG):
                    total = total + totals[kind, i, c * step_of + e].astype(jnp.float32)
                kvo[kind, c * step_of + e] = total.astype(jnp.bfloat16)
                return carry

            lax.fori_loop(0, step_of, one_sum, 0)
        for e in range(step_of):
            for kind in range(2):
                deliver(kind, c * step_of + rem(e + line[kind], step_of)).start()

    for m in range(CH):
        for kind in range(2):
            delivered(kind, m).wait_recv()

    sibling = device(rg, column, 1 - core)
    half = BLOCK // HALVES

    def half_rows(q):
        return pl.ds(pl.multiple_of(q * half, half), half)

    def chip(axis, i, core):
        return device(rem(rg + axis * i, RG), rem(column + (1 - axis) * i, RG), core)

    def along(q, axis, i):
        return remote(
            blk.at[0, 0, :, half_rows(q)], blk.at[3 * axis + RG - i, 0, :, half_rows(q)],
            gs.at[q, 3 * axis + i], gr.at[q, 3 * axis + RG - i, 0], ctx=chip(axis, i, core),
        )

    def across(q, spot):
        return remote(
            blk.at[spot, 0, :, half_rows(q)], blk.at[spot, 1, :, half_rows(q)],
            gs.at[q, 7 + spot], gr.at[q, spot, 1], ctx=sibling,
        )

    def arrival(q, spot, other):
        return remote(
            blk.at[spot, other, :, half_rows(q)], blk.at[spot, other, :, half_rows(q)],
            gs.at[q, 0], gr.at[q, spot, other], ctx=sibling,
        )

    ways = ((1, 3), (3, 1))

    def onward(q, axis):
        to, source = ways[q]
        return remote(
            blk.at[3 * axis + source, 0, :, half_rows(q)], blk.at[3 * axis + 2, 0, :, half_rows(q)],
            gs.at[q, 3 * axis + 2], gr.at[q, 3 * axis + 2, 0], ctx=chip(axis, to, core),
        )

    for q in range(HALVES):
        for k in range(2):
            for axis in range(2):
                along(q, axis, ways[q][k]).start()
        across(q, 0).start()

    for u in range(RG):
        @pl.when(w_source(u) != me)
        def _():
            remote(wsh, w_rows(u), wgs.at[u], wgr.at[u], ctx=w_source(u)).wait_recv()

        @pl.when(w_source(u) == me)
        def _():
            w_own().wait()

    def out_part(j, axis, v, q):
        z, y, b = div(j, CH), rem(div(j, 2), RG), rem(j, 2)
        number = (1 - axis) * device(2 * b + v, y, 0) + axis * device(z, 2 * b + v, 1)
        return out_hbm.at[half_rows(q), pl.ds(pl.multiple_of(number * shard, shard), shard)]

    def out_copy(q, axis, i, other, v):
        core_there = core + other * (1 - 2 * core)
        return remote(
            outs.at[q, axis, i, other, v], out_part(me, axis, v, q),
            os_.at[q, axis, i, other, v], or_.at[q, axis, rem(RG - i, RG), other, v], ctx=chip(axis, i, core_there),
        )

    def out_own(q, axis, v):
        return pltpu.make_async_copy(outs.at[q, axis, 0, 0, v], out_part(me, axis, v, q), own_sem.at[q, axis, v])

    def multiply(q, first, last):
        def one(m, carry):
            axis, t = rem(m, 2), div(m, 2)
            i = t + div(t, 2) * (5 - 2 * t)
            spot = jnp.where(i == 0, 0, 3 * axis + i)

            @pl.when(m != 1)
            def _():
                arrival(q, spot, 1).wait_recv()

            left = jnp.concatenate(
                [
                    jnp.concatenate([blk[spot, other, c, q * half:(q + 1) * half] for c in range(CH)], axis=1)
                    for other in range(2)
                ],
                axis=0,
            )
            right = wfull[pl.ds(pl.multiple_of(axis * 2 * shard, 2 * shard), 2 * shard)]
            product = lax.dot_general(left, right, nt, preferred_element_type=jnp.float32).astype(jnp.bfloat16)
            for other in range(2):
                for v in range(2):
                    outs[q, axis, i, other, v] = product[other * half:(other + 1) * half, v * shard:(v + 1) * shard]
            for v in range(2):
                out_copy(q, axis, i, 1, v).start()

                @pl.when(i != 0)
                def _():
                    out_copy(q, axis, i, 0, v).start()

                @pl.when(i == 0)
                def _():
                    out_own(q, axis, v).start()
            return carry

        lax.fori_loop(first, last, one, 0)

    def share(q, spots):
        for k in spots:
            for axis in range(2):
                spot = 3 * axis + (2 if k == 2 else ways[q][1 - k])
                arrival(q, spot, 0).wait_recv()
                if k == 0:
                    onward(q, axis).start()
                across(q, spot).start()

    near = 2 * RG - 2
    share(0, (0, 1))
    share(1, (0, 1))
    multiply(0, 0, near)
    share(0, (2,))
    multiply(1, 0, near)
    multiply(0, near, 2 * RG)
    share(1, (2,))
    multiply(1, near, 2 * RG)

    mates(lambda kind, m: piece_out(kind, m).wait_send())
    mates(lambda kind, m: window_out(kind, m).wait_send())
    for far in range(RG):
        for i in range(1, RG):
            for kind in range(2):
                pair_out(kind, i, far).wait_send()
    for cut in range(2):
        mates(lambda kind, m: term_out(kind, m, cut).wait_send())
    for kind in range(2):
        for m in range(CH):
            deliver(kind, m).wait_send()
        for c in range(PARTS):
            for i in range(1, RG):
                total_out(kind, i, c).wait_send()
    w_shift.wait_send()
    for z in range(RG):
        @pl.when(w_target(z) != me)
        def _():
            w_out(z).wait_send()

    for q in range(HALVES):
        for axis in range(2):
            along(q, axis, 1).wait_send()
            along(q, axis, 3).wait_send()
            onward(q, axis).wait_send()
            for i in range(1, RG):
                across(q, 3 * axis + i).wait_send()
        across(q, 0).wait_send()
    for head in range(HK):
        wide_q = pl.ds(head * GROUP * HD, GROUP * HD)
        pltpu.make_async_copy(dq_s.at[:, wide_q], dq_hbm.at[:, wide_q], dq_sem.at[head]).wait()

    def finish(m, carry):
        axis, i = div(m, RG), rem(m, RG)
        for q in range(HALVES):
            for v in range(2):
                for other in range(2):
                    there = core + other * (1 - 2 * core)
                    incoming = remote(
                        outs.at[q, axis, i, other, v], out_part(chip(axis, i, there), axis, v, q),
                        os_.at[q, axis, i, other, v], or_.at[q, axis, i, other, v], ctx=sibling,
                    )

                    @pl.when(i + other > 0)
                    def _():
                        out_copy(q, axis, i, other, v).wait_send()
                        incoming.wait_recv()

                @pl.when(i == 0)
                def _():
                    out_own(q, axis, v).wait()
        return carry

    lax.fori_loop(0, 2 * RG, finish, 0)


def shards(queries, key_rows, value_rows, out_grad, kv_weight, doc_lengths, block_plan):
    n = lax.axis_size("ctx")
    sections = lax.axis_size("section")
    tokens, width = queries.shape[1:]
    features = kv_weight.shape[1]
    model = features * n
    share = model // CH
    hbm = pl.BlockSpec(memory_space=pltpu.HBM)
    anywhere = pl.BlockSpec(memory_space=pl.ANY)
    low = jnp.bfloat16
    dma = pltpu.SemaphoreType.DMA
    query_grad, input_grad = pl.pallas_call(
        functools.partial(kernel, n, sections),
        out_shape=(
            jax.ShapeDtypeStruct((tokens, width), low),
            jax.ShapeDtypeStruct((tokens, model), low),
        ),
        in_specs=[hbm] * 7,
        out_specs=(anywhere, anywhere),
        scratch_shapes=[
            pltpu.SMEM(doc_lengths.shape, jnp.int32),
            pltpu.SMEM((n,), jnp.int32),
            pltpu.SMEM((2, n), jnp.int32),
            pltpu.VMEM((tokens, width), low),
            pltpu.VMEM((tokens, width), low),
            pltpu.VMEM((tokens, width), low),
            pltpu.VMEM((CH, SLOTS, BLOCK, HD), low),
            pltpu.VMEM((2, n, BLOCK // 2, HD), low),
            pltpu.VMEM((2, CH, BACK, BLOCK // 2, HD), low),
            pltpu.VMEM((SLOTS * BLOCK, BLOCK), jnp.float32),
            pltpu.VMEM((SLOTS * BLOCK, GROUP * BLOCK), jnp.float32),
            pltpu.VMEM((SLOTS * BLOCK, GROUP * BLOCK), jnp.float32),
            pltpu.VMEM((CH, SLOTS, BLOCK, HD), low),
            pltpu.VMEM((2, CH + 1, SLOTS, BLOCK // 2, HD), low),
            pltpu.VMEM((2, n, BLOCK // 2, HD), low),
            pltpu.VMEM((2, RG, CH, BLOCK // 2, HD), low),
            pltpu.VMEM((2, CH, BLOCK // 2, HD), low),
            pltpu.VMEM((7, 2, CH, BLOCK, HD), low),
            pltpu.VMEM((features, CH * HD), low),
            pltpu.VMEM((share, CH * HD), low),
            pltpu.VMEM((HALVES, 2, RG, 2, 2, BLOCK // HALVES, features), low),
            dma((4,)), dma((2, HK)), dma((HK,)),
            dma((2, CH)), dma((2, CH)), dma((2, RG, RG)), dma((2, RG, RG)), dma((2, CH)), dma((2, CH)),
            dma((2, CH, 2)), dma((2, CH, 2)),
            dma((2, RG, PARTS)), dma((2, RG, PARTS)), dma((2, CH)), dma((2, CH)),
            dma((HALVES, 14)), dma((HALVES, 7, 2)),
            dma((HALVES, 2, RG, 2, 2)), dma((HALVES, 2, RG, 2, 2)), dma((2, 2)), dma((HALVES, 2, 2)),
            pltpu.SemaphoreType.REGULAR, dma((7,)), dma, dma, dma((RG,)), dma((RG,)),
        ],
        compiler_params=pltpu.CompilerParams(
            collective_id=0, has_side_effects=True, vmem_limit_bytes=56 * 1024 * 1024
        ),
    )(doc_lengths, block_plan, queries[0], key_rows[0], value_rows[0], out_grad[0], kv_weight[0])
    return (query_grad[None], input_grad[None])


def solution(mesh):
    spec = P("section", "ctx", None)
    return jax.shard_map(
        shards, mesh=mesh, in_specs=(spec,) * 5 + (P(), P()), out_specs=(spec, spec), check_vma=False
    )
```

```python
import functools
import math

import jax
import jax.numpy as jnp
from jax import lax
from jax.experimental import pallas as pl
from jax.experimental.pallas import tpu as pltpu
from jax.sharding import PartitionSpec as P

HQ = 32
HK = 4
HD = 128
BLOCK = 128
GROUP = HQ // HK
BACK = 8
SLOTS = BACK + 1
CH = 2 * HK
SUB = 32
RG = BLOCK // SUB
MASKED = -1e30
MIX = 13
EARLY = 6
PARTS = 2
HALVES = 2
KEYS = 384
MESH = pl.DeviceIdType.MESH


def rem(a, b):
    return lax.rem(a, b)


def div(a, b):
    return lax.div(a, b)


def kernel(
    n, sections, lens_hbm, plan_hbm, q_hbm, k_hbm, v_hbm, o_hbm, w_hbm, dq_hbm, out_hbm,
    lens, plan, inv, q_s, o_s, dq_s, kvw, hold, send2, bias, s_s, g_s, part, terms, sums, totals, kvo, blk, wsh, wfull, outs,
    in_sem, kv_sem, dq_sem, s1s, s1r, g1s, g1r, s2s, s2r, s3s, s3r, rs, rr, ds_, dr, gs, gr, os_, or_, own_terms, own_sem, ready, loc_sem, wxs, wxr, wgs, wgr,
):
    me = lax.axis_index("ctx")
    sec = lax.axis_index("section")
    rg = div(me, CH)
    ch = rem(me, CH)
    core = rem(ch, 2)
    column = div(ch, 2)
    before = rem(sec + sections - 1, sections)

    def remote(src, dst, send, recv, **where):
        return pltpu.make_async_remote_copy(
            src_ref=src, dst_ref=dst, send_sem=send, recv_sem=recv,
            device_id=where, device_id_type=MESH,
        )

    load_lens = pltpu.make_async_copy(lens_hbm, lens, in_sem.at[2])
    load_plan = pltpu.make_async_copy(plan_hbm, plan, in_sem.at[3])
    load_q = pltpu.make_async_copy(q_hbm, q_s, in_sem.at[0])
    load_o = pltpu.make_async_copy(o_hbm, o_s, in_sem.at[1])
    load_kv = [
        pltpu.make_async_copy(
            (v_hbm if kind else k_hbm).at[:, pl.ds(head * HD, HD)], kvw.at[kind * HK + head, BACK], kv_sem.at[kind, head]
        )
        for kind in range(2)
        for head in range(HK)
    ]
    for load in (load_plan, load_lens, *load_kv, load_q, load_o):
        load.start()

    def device(z, y, core):
        return z * CH + 2 * y + core

    halves = BLOCK // 2
    line = (2 * column + core, 2 * rg + core)

    def mate(kind, m):
        return device(rg, div(m, 2), rem(m, 2)) if kind == 0 else device(div(m, 2), column, rem(m, 2))

    barrier = pltpu.get_barrier_semaphore()

    def greet(j):
        pl.semaphore_signal(barrier, inc=1, device_id={"ctx": j}, device_id_type=MESH)

    for k in range(1, CH):
        greet(mate(0, rem(line[0] + k, CH)))
    for k in range(1, RG):
        for there in range(2):
            greet(device(rem(rg + k, RG), column, there))
    after = rem(sec + 1, sections)
    for neighbour in (before, after):
        pl.semaphore_signal(barrier, inc=1, device_id={"section": neighbour}, device_id_type=MESH)
    load_plan.wait()
    load_lens.wait()

    def invert(b, carry):
        place = jnp.int32(0)
        for p in range(n):
            place = jnp.where(plan[p] == b, p, place)
        inv[0, b] = place
        inv[1, b] = rem(div(place, 2), RG) * CH + div(place, CH) * 2 + rem(place, 2)
        return carry

    lax.fori_loop(0, n, invert, 0)
    for load in load_kv:
        load.wait()
    pl.semaphore_wait(barrier, CH - 1 + 2 * (RG - 1) + 2)
    pl.semaphore_signal(ready, inc=1, device_id={"section": after}, device_id_type=MESH)

    def held_head(m):
        return rem(div(m, 2) + 2 * rem(m, 2), HK)

    def half_of(m):
        return pl.ds(pl.multiple_of(rem(m, 2) * halves, halves), halves)

    held = (me, column * CH + 2 * rg + core)

    def piece_out(kind, m):
        return remote(
            kvw.at[kind * HK + held_head(m), BACK, half_of(m)], hold.at[kind, held[kind]],
            s1s.at[kind, m], s1r.at[kind, line[kind]], ctx=mate(kind, m),
        )

    def piece_in(kind, m):
        return remote(
            kvw.at[0, BACK, half_of(0)], hold.at[kind, m if kind else rg * CH + m],
            s1s.at[kind, m], s1r.at[kind, m], ctx=mate(kind, m),
        )

    def mates(body):
        for k in range(1, CH):
            for kind in range(2):
                body(kind, rem(line[kind] + 3 * k, CH))

    for far in (0, 1, 3, 2):
        for there in ((1,) if far == 0 else (0, 1)):
            for kind in range(2):
                piece_out(kind, 2 * rem((rg if kind else column) + far, RG) + rem(core + there, 2)).start()
    w_shift = remote(w_hbm, wsh, wxs, wxr, section=before)
    w_shift.start()
    for kind in range(2):
        hold[kind, held[kind]] = kvw[kind * HK + held_head(line[kind]), BACK, half_of(line[kind])]

    token_block = plan[me]
    row_token = token_block * BLOCK + lax.broadcasted_iota(jnp.int32, (1, BLOCK), 1)
    start = jnp.zeros((1, BLOCK), jnp.int32)
    end = jnp.int32(0)
    for j in range(lens.shape[0]):
        end = end + lens[j]
        start = jnp.where(row_token >= end, end, start)
    key_token = (token_block - BACK) * BLOCK + lax.broadcasted_iota(jnp.int32, (SLOTS * BLOCK, BLOCK), 0)
    seen = jnp.logical_and(key_token >= start, key_token <= row_token)
    bias[...] = jnp.where(seen, 0.0, MASKED)
    for kind in range(2):
        terms[kind, CH] = jnp.zeros((SLOTS, halves, HD), jnp.bfloat16)

    def pair(kind, i, far):
        here, along_it = (rg, column) if kind == 0 else (column, rg)
        first = rem(here + i, RG) * CH + 2 * rem(along_it + far, RG)
        return hold.at[kind, pl.ds(pl.multiple_of(first, 2), 2)]

    def peer(kind, i):
        return device(rem(rg + i, RG), column, core) if kind == 0 else device(rg, rem(column + i, RG), core)

    def pair_out(kind, i, far):
        return remote(
            pair(kind, 0, far), pair(kind, 0, far), g1s.at[kind, i, far], g1r.at[kind, RG - i, far], ctx=peer(kind, i)
        )

    def pair_in(kind, i, far):
        return remote(
            pair(kind, i, far), pair(kind, i, far), g1s.at[kind, i, far], g1r.at[kind, i, far], ctx=peer(kind, i)
        )

    def came_from(kind, far, there):
        return 2 * rem((column if kind == 0 else rg) + far, RG) + there

    for far in (0, 1, 3, 2):
        for kind in range(2):
            if far:
                piece_in(kind, came_from(kind, far, core)).wait_recv()
            piece_in(kind, came_from(kind, far, 1 - core)).wait_recv()
            for i in (1, 3, 2):
                pair_out(kind, i, far).start()
    for far in (0, 1, 3, 2):
        for i in (1, 3, 2):
            for kind in range(2):
                pair_in(kind, i, far).wait_recv()

    def window_slots(kind, m):
        return kvw.at[kind * HK + held_head(m), pl.ds(0, BACK), half_of(m)]

    def window_out(kind, m):
        return remote(
            send2.at[kind, m], window_slots(kind, line[kind]), s2s.at[kind, m], s2r.at[kind, line[kind]], ctx=mate(kind, m)
        )

    def window_own(kind):
        return pltpu.make_async_copy(send2.at[kind, line[kind]], window_slots(kind, line[kind]), loc_sem.at[4 * kind])

    def window_in(kind, m):
        return remote(send2.at[kind, m], window_slots(kind, m), s2s.at[kind, m], s2r.at[kind, m], ctx=mate(kind, m))

    turn_of = rem(rg + column, HK)

    def window_step(i, carry):
        for kind in range(2):
            start_at = held_head(line[kind]) + 2 * RG - div(i, 2) - (rg if kind == 0 else column)
            m = 2 * rem(start_at, RG) + rem(i, 2)
            first = plan[mate(kind, m)] - BACK
            for w in range(BACK):
                send2[kind, m, w] = hold[kind, inv[kind, jnp.maximum(first + w, 0)]]

            @pl.when(m != line[kind])
            def _():
                window_out(kind, m).start()

            @pl.when(m == line[kind])
            def _():
                window_own(kind).start()
        return carry

    lax.fori_loop(0, CH, window_step, 0)

    place = rg * (1 - core) + column * core
    w_slot = 2 * core + rem(place, 2)
    shard = w_hbm.shape[0]

    def w_rows(slot):
        return wfull.at[pl.ds(pl.multiple_of(slot * shard, shard), shard)]

    def w_target(i):
        return device(i * (1 - core) + rg * core, column * (1 - core) + i * core, div(place, 2))

    def w_source(u):
        if u < 2:
            return device(2 * core + u, column, 0)
        return device(rg, 2 * core + u - 2, 1)

    def w_out(i):
        return remote(wsh, w_rows(w_slot), wgs.at[i], wgr.at[w_slot], ctx=w_target(i))

    def w_own():
        return pltpu.make_async_copy(wsh, w_rows(w_slot), loc_sem.at[1])

    def spread_weights():
        w_shift.wait_recv()
        for z in range(RG):
            @pl.when(w_target(z) != me)
            def _():
                w_out(z).start()

            @pl.when(w_target(z) == me)
            def _():
                w_own().start()

    load_q.wait()
    load_o.wait()

    scale = 1.0 / math.sqrt(HD)
    power = scale * math.log2(math.e)
    nt = (((1,), (1,)), ((), ()))
    tn = (((0,), (0,)), ((), ()))

    cuts = (pl.ds(0, EARLY), pl.ds(EARLY, SLOTS - EARLY))

    def term_out(kind, m, cut):
        return remote(
            part.at[kind * HK + held_head(m), cuts[cut], half_of(m)], terms.at[kind, line[kind], cuts[cut]],
            s3s.at[kind, m, cut], s3r.at[kind, line[kind], cut], ctx=mate(kind, m),
        )

    def term_own(kind, cut):
        m = line[kind]
        return pltpu.make_async_copy(
            part.at[kind * HK + held_head(m), cuts[cut], half_of(m)], terms.at[kind, m, cuts[cut]], own_terms.at[kind, cut]
        )

    def term_in(kind, m, cut):
        return remote(
            part.at[0, cuts[cut], half_of(0)], terms.at[kind, m, cuts[cut]],
            s3s.at[kind, m, cut], s3r.at[kind, m, cut], ctx=mate(kind, m),
        )

    def send_terms(head, cut):
        for half in range(2):
            m = 2 * rem(head + RG - 2 * half, RG) + half
            for kind in range(2):
                @pl.when(m != line[kind])
                def _():
                    term_out(kind, m, cut).start()

                @pl.when(m == line[kind])
                def _():
                    term_own(kind, cut).start()

    def one_head(step, carry):
        head = rem(step + turn_of, HK)
        for half in range(2):
            m = 2 * rem(head + RG - 2 * half, RG) + half
            for kind in range(2):
                @pl.when(m != line[kind])
                def _():
                    window_in(kind, m).wait_recv()

                @pl.when(m == line[kind])
                def _():
                    window_own(kind).wait()

        def columns(i):
            return pl.ds(pl.multiple_of((head * GROUP + i) * HD, HD), HD)

        q2 = jnp.concatenate([q_s[:, columns(i)] for i in range(GROUP)], axis=0)
        o2 = jnp.concatenate([o_s[:, columns(i)] for i in range(GROUP)], axis=0)
        wide = GROUP * BLOCK
        spans = [(slice(i, i + KEYS), slice(i // BLOCK, (i + KEYS) // BLOCK)) for i in range(0, SLOTS * BLOCK, KEYS)]

        def folded(x, over):
            return over(x.reshape(KEYS // 8, 8, wide), axis=0)

        peak = None
        for span, slots in spans:
            b = bias[span]
            keys = kvw[head, slots].reshape(KEYS, HD)
            scores = lax.dot_general(keys, q2, nt, preferred_element_type=jnp.float32)
            scores = scores + jnp.concatenate([b] * GROUP, axis=1)
            s_s[span] = scores
            top = folded(scores, jnp.max)
            peak = top if peak is None else jnp.maximum(peak, top)
        peak = jnp.max(peak, axis=0, keepdims=True)
        total = jnp.zeros((8, wide), jnp.float32)
        weighted = jnp.zeros((8, wide), jnp.float32)
        for span, slots in spans:
            terms = jnp.exp2((s_s[span] - peak) * power)
            s_s[span] = terms
            total = total + folded(terms, jnp.sum)
            values = kvw[HK + head, slots].reshape(KEYS, HD)
            grads = lax.dot_general(values, o2, nt, preferred_element_type=jnp.float32)
            g_s[span] = grads
            weighted = weighted + folded(terms * grads, jnp.sum)
        inverse = 1.0 / jnp.sum(total, axis=0, keepdims=True)
        delta = jnp.sum(weighted, axis=0, keepdims=True) * inverse
        dq = jnp.zeros((wide, HD), jnp.float32)
        for span, slots in spans:
            prob = s_s[span] * inverse
            prob_low = prob.astype(jnp.bfloat16)
            score_low = (prob * (g_s[span] - delta)).astype(jnp.bfloat16)
            dv = jnp.dot(prob_low, o2, preferred_element_type=jnp.float32)
            dk = jnp.dot(score_low, q2, preferred_element_type=jnp.float32) * scale
            part[HK + head, slots] = dv.astype(jnp.bfloat16).reshape(KEYS // BLOCK, BLOCK, HD)
            part[head, slots] = dk.astype(jnp.bfloat16).reshape(KEYS // BLOCK, BLOCK, HD)
            keys = kvw[head, slots].reshape(KEYS, HD)
            dq = dq + lax.dot_general(score_low, keys, tn, preferred_element_type=jnp.float32)
            if slots.stop == EARLY:
                send_terms(head, 0)
        for i in range(GROUP):
            dq_s[:, columns(i)] = (dq[i * BLOCK:(i + 1) * BLOCK] * scale).astype(jnp.bfloat16)

        send_terms(head, 1)
        wide = pl.ds(pl.multiple_of(head * GROUP * HD, GROUP * HD), GROUP * HD)
        pltpu.make_async_copy(dq_s.at[:, wide], dq_hbm.at[:, wide], dq_sem.at[head]).start()
        return carry

    spread_weights()
    lax.fori_loop(0, HK, one_head, 0)

    for cut in range(2):
        mates(lambda kind, m: term_in(kind, m, cut).wait_recv())
        for kind in range(2):
            term_own(kind, cut).wait()

    step_of = CH // PARTS

    def some(first, part_no):
        return pl.ds(pl.multiple_of(first * CH + part_no * step_of, step_of), step_of)

    def total_out(kind, i, c):
        to = rem((rg if kind == 0 else column) + i, RG)
        return remote(
            sums.at[kind, some(to, c)], totals.at[kind, RG - i, some(0, c)],
            rs.at[kind, i, c], rr.at[kind, RG - i, c], ctx=peer(kind, i),
        )

    def total_in(kind, i, c):
        return remote(
            sums.at[kind, some(0, c)], totals.at[kind, i, some(0, c)], rs.at[kind, i, c], rr.at[kind, i, c], ctx=peer(kind, i)
        )

    for c in range(PARTS):
        for i in (2, 1, 3, 0):
            for kind in range(2):
                here = rg if kind == 0 else column
                to = rem(here + i, RG)

                def one_block(e, carry):
                    p = device(to, div(e, 2), rem(e, 2)) if kind == 0 else device(div(e, 2), to, rem(e, 2))
                    total = jnp.zeros((halves, HD), jnp.float32)
                    for w in range(SLOTS):
                        later = plan[p] + BACK - w
                        source = inv[kind, jnp.minimum(later, n - 1)]
                        wanted = jnp.logical_and(later < n, div(source, CH) == here)
                        total = total + terms[kind, jnp.where(wanted, rem(source, CH), CH), w].astype(jnp.float32)
                    sums[kind, to * CH + e] = total.astype(jnp.bfloat16)
                    return carry

                lax.fori_loop(c * step_of, (c + 1) * step_of, one_block, 0)
                if i > 0:
                    total_out(kind, i, c).start()

    def owned(kind, m):
        return blk.at[0, 0, kind * HK + held_head(m), half_of(m)]

    def deliver(kind, m):
        return remote(
            kvo.at[kind, m], owned(kind, line[kind]), ds_.at[kind, m], dr.at[kind, line[kind]],
            section=before, ctx=mate(kind, m),
        )

    def delivered(kind, m):
        return remote(kvo.at[kind, m], owned(kind, m), ds_.at[kind, m], dr.at[kind, m], section=before, ctx=mate(kind, m))

    pl.semaphore_wait(ready, 1)
    for c in range(PARTS):
        for kind in range(2):
            here = rg if kind == 0 else column
            for i in range(1, RG):
                total_in(kind, i, c).wait_recv()

            def one_sum(e, carry):
                total = sums[kind, here * CH + c * step_of + e].astype(jnp.float32)
                for i in range(1, RG):
                    total = total + totals[kind, i, c * step_of + e].astype(jnp.float32)
                kvo[kind, c * step_of + e] = total.astype(jnp.bfloat16)
                return carry

            lax.fori_loop(0, step_of, one_sum, 0)
        for e in range(step_of):
            for kind in range(2):
                deliver(kind, c * step_of + rem(e + line[kind], step_of)).start()

    for m in range(CH):
        for kind in range(2):
            delivered(kind, m).wait_recv()

    sibling = device(rg, column, 1 - core)
    half = BLOCK // HALVES

    def half_rows(q):
        return pl.ds(pl.multiple_of(q * half, half), half)

    def chip(axis, i, core):
        return device(rem(rg + axis * i, RG), rem(column + (1 - axis) * i, RG), core)

    def along(q, axis, i):
        return remote(
            blk.at[0, 0, :, half_rows(q)], blk.at[3 * axis + RG - i, 0, :, half_rows(q)],
            gs.at[q, 3 * axis + i], gr.at[q, 3 * axis + RG - i, 0], ctx=chip(axis, i, core),
        )

    def across(q, spot):
        return remote(
            blk.at[spot, 0, :, half_rows(q)], blk.at[spot, 1, :, half_rows(q)],
            gs.at[q, 7 + spot], gr.at[q, spot, 1], ctx=sibling,
        )

    def arrival(q, spot, other):
        return remote(
            blk.at[spot, other, :, half_rows(q)], blk.at[spot, other, :, half_rows(q)],
            gs.at[q, 0], gr.at[q, spot, other], ctx=sibling,
        )

    ways = ((1, 3), (3, 1))

    def onward(q, axis):
        to, source = ways[q]
        return remote(
            blk.at[3 * axis + source, 0, :, half_rows(q)], blk.at[3 * axis + 2, 0, :, half_rows(q)],
            gs.at[q, 3 * axis + 2], gr.at[q, 3 * axis + 2, 0], ctx=chip(axis, to, core),
        )

    for q in range(HALVES):
        for k in range(2):
            for axis in range(2):
                along(q, axis, ways[q][k]).start()
        across(q, 0).start()

    for u in range(RG):
        @pl.when(w_source(u) != me)
        def _():
            remote(wsh, w_rows(u), wgs.at[u], wgr.at[u], ctx=w_source(u)).wait_recv()

        @pl.when(w_source(u) == me)
        def _():
            w_own().wait()

    def out_part(j, axis, v, q):
        z, y, b = div(j, CH), rem(div(j, 2), RG), rem(j, 2)
        number = (1 - axis) * device(2 * b + v, y, 0) + axis * device(z, 2 * b + v, 1)
        return out_hbm.at[half_rows(q), pl.ds(pl.multiple_of(number * shard, shard), shard)]

    def out_copy(q, axis, i, other, v):
        core_there = core + other * (1 - 2 * core)
        return remote(
            outs.at[q, axis, i, other, v], out_part(me, axis, v, q),
            os_.at[q, axis, i, other, v], or_.at[q, axis, rem(RG - i, RG), other, v], ctx=chip(axis, i, core_there),
        )

    def out_own(q, axis, v):
        return pltpu.make_async_copy(outs.at[q, axis, 0, 0, v], out_part(me, axis, v, q), own_sem.at[q, axis, v])

    def multiply(q, first, last):
        def one(m, carry):
            axis, t = rem(m, 2), div(m, 2)
            i = t + div(t, 2) * (5 - 2 * t)
            spot = jnp.where(i == 0, 0, 3 * axis + i)

            @pl.when(m != 1)
            def _():
                arrival(q, spot, 1).wait_recv()

            left = jnp.concatenate(
                [
                    jnp.concatenate([blk[spot, other, c, q * half:(q + 1) * half] for c in range(CH)], axis=1)
                    for other in range(2)
                ],
                axis=0,
            )
            right = wfull[pl.ds(pl.multiple_of(axis * 2 * shard, 2 * shard), 2 * shard)]
            product = lax.dot_general(left, right, nt, preferred_element_type=jnp.float32).astype(jnp.bfloat16)
            for other in range(2):
                for v in range(2):
                    outs[q, axis, i, other, v] = product[other * half:(other + 1) * half, v * shard:(v + 1) * shard]
            for v in range(2):
                out_copy(q, axis, i, 1, v).start()

                @pl.when(i != 0)
                def _():
                    out_copy(q, axis, i, 0, v).start()

                @pl.when(i == 0)
                def _():
                    out_own(q, axis, v).start()
            return carry

        lax.fori_loop(first, last, one, 0)

    def share(q, spots):
        for k in spots:
            for axis in range(2):
                spot = 3 * axis + (2 if k == 2 else ways[q][1 - k])
                arrival(q, spot, 0).wait_recv()
                if k == 0:
                    onward(q, axis).start()
                across(q, spot).start()

    near = 2 * RG - 2
    share(0, (0, 1))
    share(1, (0, 1))
    multiply(0, 0, near)
    share(0, (2,))
    multiply(1, 0, near)
    multiply(0, near, 2 * RG)
    share(1, (2,))
    multiply(1, near, 2 * RG)

    mates(lambda kind, m: piece_out(kind, m).wait_send())
    mates(lambda kind, m: window_out(kind, m).wait_send())
    for far in range(RG):
        for i in range(1, RG):
            for kind in range(2):
                pair_out(kind, i, far).wait_send()
    for cut in range(2):
        mates(lambda kind, m: term_out(kind, m, cut).wait_send())
    for kind in range(2):
        for m in range(CH):
            deliver(kind, m).wait_send()
        for c in range(PARTS):
            for i in range(1, RG):
                total_out(kind, i, c).wait_send()
    w_shift.wait_send()
    for z in range(RG):
        @pl.when(w_target(z) != me)
        def _():
            w_out(z).wait_send()

    for q in range(HALVES):
        for axis in range(2):
            along(q, axis, 1).wait_send()
            along(q, axis, 3).wait_send()
            onward(q, axis).wait_send()
            for i in range(1, RG):
                across(q, 3 * axis + i).wait_send()
        across(q, 0).wait_send()
    for head in range(HK):
        wide_q = pl.ds(head * GROUP * HD, GROUP * HD)
        pltpu.make_async_copy(dq_s.at[:, wide_q], dq_hbm.at[:, wide_q], dq_sem.at[head]).wait()

    def finish(m, carry):
        axis, i = div(m, RG), rem(m, RG)
        for q in range(HALVES):
            for v in range(2):
                for other in range(2):
                    there = core + other * (1 - 2 * core)
                    incoming = remote(
                        outs.at[q, axis, i, other, v], out_part(chip(axis, i, there), axis, v, q),
                        os_.at[q, axis, i, other, v], or_.at[q, axis, i, other, v], ctx=sibling,
                    )

                    @pl.when(i + other > 0)
                    def _():
                        out_copy(q, axis, i, other, v).wait_send()
                        incoming.wait_recv()

                @pl.when(i == 0)
                def _():
                    out_own(q, axis, v).wait()
        return carry

    lax.fori_loop(0, 2 * RG, finish, 0)


def shards(queries, key_rows, value_rows, out_grad, kv_weight, doc_lengths, block_plan):
    n = lax.axis_size("ctx")
    sections = lax.axis_size("section")
    tokens, width = queries.shape[1:]
    features = kv_weight.shape[1]
    model = features * n
    share = model // CH
    hbm = pl.BlockSpec(memory_space=pltpu.HBM)
    anywhere = pl.BlockSpec(memory_space=pl.ANY)
    low = jnp.bfloat16
    dma = pltpu.SemaphoreType.DMA
    query_grad, input_grad = pl.pallas_call(
        functools.partial(kernel, n, sections),
        out_shape=(
            jax.ShapeDtypeStruct((tokens, width), low),
            jax.ShapeDtypeStruct((tokens, model), low),
        ),
        in_specs=[hbm] * 7,
        out_specs=(anywhere, anywhere),
        scratch_shapes=[
            pltpu.SMEM(doc_lengths.shape, jnp.int32),
            pltpu.SMEM((n,), jnp.int32),
            pltpu.SMEM((2, n), jnp.int32),
            pltpu.VMEM((tokens, width), low),
            pltpu.VMEM((tokens, width), low),
            pltpu.VMEM((tokens, width), low),
            pltpu.VMEM((CH, SLOTS, BLOCK, HD), low),
            pltpu.VMEM((2, n, BLOCK // 2, HD), low),
            pltpu.VMEM((2, CH, BACK, BLOCK // 2, HD), low),
            pltpu.VMEM((SLOTS * BLOCK, BLOCK), jnp.float32),
            pltpu.VMEM((SLOTS * BLOCK, GROUP * BLOCK), jnp.float32),
            pltpu.VMEM((SLOTS * BLOCK, GROUP * BLOCK), jnp.float32),
            pltpu.VMEM((CH, SLOTS, BLOCK, HD), low),
            pltpu.VMEM((2, CH + 1, SLOTS, BLOCK // 2, HD), low),
            pltpu.VMEM((2, n, BLOCK // 2, HD), low),
            pltpu.VMEM((2, RG, CH, BLOCK // 2, HD), low),
            pltpu.VMEM((2, CH, BLOCK // 2, HD), low),
            pltpu.VMEM((7, 2, CH, BLOCK, HD), low),
            pltpu.VMEM((features, CH * HD), low),
            pltpu.VMEM((share, CH * HD), low),
            pltpu.VMEM((HALVES, 2, RG, 2, 2, BLOCK // HALVES, features), low),
            dma((4,)), dma((2, HK)), dma((HK,)),
            dma((2, CH)), dma((2, CH)), dma((2, RG, RG)), dma((2, RG, RG)), dma((2, CH)), dma((2, CH)),
            dma((2, CH, 2)), dma((2, CH, 2)),
            dma((2, RG, PARTS)), dma((2, RG, PARTS)), dma((2, CH)), dma((2, CH)),
            dma((HALVES, 14)), dma((HALVES, 7, 2)),
            dma((HALVES, 2, RG, 2, 2)), dma((HALVES, 2, RG, 2, 2)), dma((2, 2)), dma((HALVES, 2, 2)),
            pltpu.SemaphoreType.REGULAR, dma((7,)), dma, dma, dma((RG,)), dma((RG,)),
        ],
        compiler_params=pltpu.CompilerParams(
            collective_id=0, has_side_effects=True, vmem_limit_bytes=56 * 1024 * 1024
        ),
    )(doc_lengths, block_plan, queries[0], key_rows[0], value_rows[0], out_grad[0], kv_weight[0])
    return (query_grad[None], input_grad[None])


def solution(mesh):
    spec = P("section", "ctx", None)
    return jax.shard_map(
        shards, mesh=mesh, in_specs=(spec,) * 5 + (P(), P()), out_specs=(spec, spec), check_vma=False
    )
```
